32 devices in a mesh: seq: 8 (over z, y), section: 4 (over x, core).
Axes of the slice: x: 2, y: 2, z: 4, core: 2. Of those that a mesh axis runs over, the one named last changes fastest.
Arguments:
- acts: bfloat16 [2048, 1408], P('seq'), may hold values from -6 to 6
- pre_act: bfloat16 [2048, 1536], P('seq', 'section'), may hold values from -6 to 6
- emb_grad: bfloat16 [1024, 1536], P('seq', 'section'), may hold values from -6 to 6
- filters: bfloat16 [7040, 1536], P('seq', 'section'), may hold values from -0.0625 to 0.0625
Outputs:
- input_grad: bfloat16 [2048, 1408], P('seq', 'section')
- filter_grad: float32 [7040, 1536], P('seq', 'section')
The draws below stay inside these ranges and needn't reach their ends.
All inputs are finite; a program needn't handle non-finite values.
Results may differ from the reference program's by a relative error of at most 0.0049.
Values may be sent and summed in bfloat16 or wider, within the bound.
No kernel may reach another device: no remote copies, remote signals or barrier semaphores. Data moves between devices by JAX's collectives and lax.ppermute only.
A program may use at most 128 MiB of HBM per device.

```python
import jax
import jax.numpy as jnp
from jax import lax

C_IN = 1408
C_OUT = 1536
KERNEL = 5
SEQS = 1
ROWS = 2048
LENGTH = 2048
EMB_ROWS = 1024


def spiked(result, own_key, source, target, blocks, factor):
    owner, partner = [(jnp.arange(result.shape[position]) // (result.shape[position] // blocks)).reshape([-1 if axis == position else 1 for axis in range(result.ndim)]) for position in (source, target)]
    chosen = jax.random.permutation(own_key, blocks)[partner]
    strong = (owner == chosen) | (owner == (partner + blocks // 2) % blocks)
    return jnp.where(strong, factor * result, result)


def shard_levels(rng, extent, cuts, low, top_value):
    def one(dim, shards_of):
        draws = jax.random.uniform(jax.random.fold_in(jax.random.fold_in(rng, 6), dim), (shards_of,), jnp.float32, low / len(cuts), top_value / len(cuts))
        return jnp.repeat(jnp.exp(draws), extent[dim] // shards_of).reshape((-1,) + (1,) * (len(extent) - dim - 1))

    level = one(*cuts[0])
    for cut in cuts[1:]:
        level = level * one(*cut)
    return level


def scatter_about(rng, extent, spread, limit, shards=(), dtype=jnp.bfloat16):
    values = spread * jax.random.normal(rng, extent, jnp.float32)
    if shards:
        values = values * shard_levels(rng, extent, shards, -0.22, 0.18)
    return jnp.clip(values, -limit, limit).astype(dtype)


def bell_draw_with(key, shape, spread, reach, cuts, heavy, dtype=jnp.bfloat16):
    entries = spread * jax.random.normal(key, shape, jnp.float32)
    if cuts:
        entries = entries * shard_levels(key, shape, cuts, -0.22, 0.18)
    return jnp.clip(spiked(entries, jax.random.fold_in(key, 3), *heavy), -reach, reach).astype(dtype)


def setup_inputs(seed: int = 0) -> dict:
    seeds = jax.random.split(jax.random.key(seed), 5)
    acts = bell_draw_with(seeds[0], (ROWS, C_IN), 1.0, 6.0, ((0, 8),), (0, 1, 8, 2.0))
    pre_act = scatter_about(seeds[1], (ROWS, C_OUT), 1.5, 6.0, ((0, 8), (1, 4)))
    emb_grad = scatter_about(seeds[2], (EMB_ROWS, C_OUT), 1.0, 6.0, ((0, 8), (1, 4)))
    filters = scatter_about(seeds[3], (KERNEL * C_IN, C_OUT), (KERNEL * C_IN) ** -0.5, 0.0625, ((0, 8), (1, 4)))
    return dict(acts=acts, pre_act=pre_act, emb_grad=emb_grad, filters=filters)


def gelu_slope(value):
    cumul = 0.5 * (1.0 + lax.erf(value * 0.7071067811865476))
    dens = jnp.exp(-0.5 * value * value) * 0.3989422804014327
    return cumul + value * dens

def reference(acts, pre_act, emb_grad, filters):
    upward = jnp.repeat(emb_grad.astype(jnp.float32), 2, axis=0) * 0.5
    zvalue = pre_act.astype(jnp.float32)
    dz_grad = (upward * gelu_slope(zvalue)).astype(jnp.bfloat16)
    act_pad = jnp.pad(acts.reshape(SEQS, LENGTH, C_IN), ((0, 0), (2, 2), (0, 0)))
    grad_pad = jnp.pad(dz_grad.reshape(SEQS, LENGTH, C_OUT), ((0, 0), (2, 2), (0, 0)))
    taps_w = filters.reshape(KERNEL, C_IN, C_OUT)
    pieces = []
    input_acc = jnp.zeros((ROWS, C_IN), jnp.float32)
    for k in range(KERNEL):
        window = act_pad[:, k:k + LENGTH].reshape(ROWS, C_IN)
        pieces.append(jnp.dot(window.T, dz_grad, preferred_element_type=jnp.float32))
        shifted = grad_pad[:, 4 - k:4 - k + LENGTH].reshape(ROWS, C_OUT)
        input_acc = input_acc + jnp.dot(shifted, taps_w[k].T, preferred_element_type=jnp.float32)
    scale_value = jnp.float32(1.0) / jnp.sqrt(jnp.float32(ROWS))
    filter_grad = jnp.concatenate(pieces, axis=0) * scale_value
    return (input_acc.astype(jnp.bfloat16), filter_grad)
```

```python
import functools
import math

import jax
import jax.numpy as jnp
from jax import lax
from jax.experimental import pallas as pl
from jax.experimental.pallas import tpu as pltpu
from jax.sharding import PartitionSpec as P

KERNEL = 5
SEQS = 1
F32 = jnp.float32
BF16 = jnp.bfloat16


def with_halo(shard, sides, width):
    for axis, dim in sides:
        size, length = (lax.axis_size(axis), shard.shape[dim])
        up = [(i, (i + 1) % size) for i in range(size - 1)]
        down = [(j, i) for i, j in up]
        last = lax.slice_in_dim(shard, length - width, length, axis=dim)
        first = lax.slice_in_dim(shard, 0, width, axis=dim)
        before = lax.ppermute(last, axis, up)
        after = lax.ppermute(first, axis, down)
        shard = jnp.concatenate([before, shard, after], axis=dim)
    return shard


def gelu_slope(value):
    cumul = 0.5 * (1.0 + lax.erf(value * 0.7071067811865476))
    dens = jnp.exp(-0.5 * value * value) * 0.3989422804014327
    return cumul + value * dens


def dz_block(pre_act, emb_grad):
    upward = jnp.repeat(emb_grad.astype(F32), 2, axis=0) * 0.5
    return (upward * gelu_slope(pre_act.astype(F32))).astype(BF16)


def shards_any(acts, pre_act, emb_grad, filters):
    rows = acts.shape[0]
    c_in = acts.shape[1]
    dz_grad = dz_block(pre_act, emb_grad)
    total_rows = rows * lax.axis_size("seq")
    length = total_rows // SEQS
    first = lax.axis_index("seq") * rows
    positions = first - 2 + jnp.arange(rows + 4, dtype=jnp.int32)
    inside = (jnp.floor_divide(positions, length) == first // length).astype(BF16)[:, None]
    scale_value = 1.0 / math.sqrt(total_rows)
    grad_rim = with_halo(dz_grad, (("seq", 0),), 2) * inside
    whole_term = (
        jnp.concatenate(
            [
                jnp.einsum(
                    "rc,ro->co",
                    acts,
                    grad_rim[4 - k : 4 - k + rows],
                    preferred_element_type=F32,
                )
                for k in range(KERNEL)
            ],
            axis=0,
        )
        * scale_value
    )
    piece = lax.all_gather(filters, "seq", axis=0, tiled=True)
    width = piece.shape[0]
    product = jnp.einsum("ro,no->rn", grad_rim, piece, preferred_element_type=F32)
    tap_of = jnp.arange(width, dtype=jnp.int32) // c_in
    total = jnp.zeros((rows, width), F32)
    for k in range(KERNEL):
        total = total + jnp.where((tap_of == k)[None, :], product[4 - k : 4 - k + rows], 0.0)
    partial_input = total.reshape(rows, KERNEL, c_in).sum(axis=1)
    input_grad = lax.psum_scatter(partial_input, "section", scatter_dimension=1, tiled=True).astype(BF16)
    filter_grad = lax.psum_scatter(whole_term, "seq", scatter_dimension=0, tiled=True)
    return (input_grad, filter_grad)


TAPS = (((0, 0), (0, 1), (1, 0), (1, 1), (2, 0)), ((2, 0), (3, 1), (3, 0), (4, 1), (4, 0)))


def coords():
    i, j = lax.axis_index("seq"), lax.axis_index("section")
    return i // 4, (i // 2) % 2, i % 2, j // 2, j % 2


def everyone(place):
    pairs = []
    for g in range(32):
        h, zl, y, x, c = (g >> 4) & 1, (g >> 3) & 1, (g >> 2) & 1, (g >> 1) & 1, g & 1
        h, zl, y, x, c = place(h, zl, y, x, c)
        pairs.append((g, h * 16 + zl * 8 + y * 4 + x * 2 + c))
    return pairs


def send(value, place):
    return lax.ppermute(value, ("seq", "section"), everyone(place))


def along_seq(value, place):
    return lax.ppermute(value, "seq", [(i, place(i)) for i in range(8)])


def in_half(value, step):
    return along_seq(value, lambda i: 4 * (i // 4) + (i % 4 + step) % 4)


SWAP_C = lambda h, zl, y, x, c: (h, zl, y, x, 1 - c)
SWAP_X = lambda h, zl, y, x, c: (h, zl, y, 1 - x, c)


def turn(a, b):
    return lambda h, zl, y, x, c: (h ^ a, c, y ^ b, x, zl)


def input_kernel(rows, unit, at, *refs):
    dz_refs, w_refs, (out_ref, dz_ref), (weights, parts) = refs[:8], refs[8:13], refs[13:15], refs[15:]
    h, zl, y, c = at[0], at[1], at[2], at[4]
    q = 2 * zl + y
    z = 2 * h + zl
    for s in range(8):
        block = 2 * lax.rem(z + 4 - s // 2, 4) + (y ^ (s % 2))
        dz_ref[pl.ds(pl.multiple_of(block * rows, rows), rows), :] = dz_refs[s][...]
    for m in range(5):
        weights[lax.rem(q + 5 - m, 5)] = w_refs[m][...]
    total = 8 * rows
    for v in range(5):
        parts[v, 0:8, :] = jnp.zeros((8, unit), F32)
        parts[v, 8 + total : 16 + total, :] = jnp.zeros((8, unit), F32)

    @pl.loop(0, 8)
    def _(t):
        start = pl.multiple_of(t * rows, rows)
        left = dz_ref[pl.ds(start, rows), :]
        for v in range(5):
            parts[v, pl.ds(start + 8, rows), :] = lax.dot_general(
                left, weights[v], (((1,), (1,)), ((), ())), preferred_element_type=F32
            )

    for half in range(2):

        @pl.when(h == half)
        def _():
            for t in range(8):
                sums = [None, None]
                for v, (tap, which) in enumerate(TAPS[half]):
                    first = 8 + t * rows + 2 - tap
                    term = parts[v, first : first + rows, :]
                    sums[which] = term if sums[which] is None else sums[which] + term
                away = ((t // 2) % 2) ^ c
                for which in range(2):
                    out_ref[away, which ^ half, 2 * (t // 4) + t % 2] = sums[which].astype(BF16)


def left_kernel(rows, unit, at, s00, s10, s01, s11, out_ref, lines):
    h, zl, y, x, c = at[0], at[1], at[2], at[3], at[4]
    for xr, cr, ref in ((0, 0, s00), (1, 0, s10), (0, 1, s01), (1, 1, s11)):
        which = x ^ xr ^ h
        for a in range(2):
            for b in range(2):
                block = 4 * (h ^ a) + 2 * (c ^ cr) + (y ^ b)
                lines[which, :, pl.ds(pl.multiple_of(block * rows, rows), rows)] = ref[2 * a + b].astype(F32).T
    total = 8 * rows
    place = lax.broadcasted_iota(jnp.int32, (unit, total), 1)
    for half in range(2):

        @pl.when(h == half)
        def _():
            for v, (tap, which) in enumerate(TAPS[half]):
                line = lines[which]
                if tap != 2:
                    line = pltpu.roll(line, (2 - tap) % total, 1)
                    fits = (place + (tap - 2) >= 0) & (place + (tap - 2) < total)
                    line = jnp.where(fits, line, 0.0)
                out_ref[v] = line.astype(BF16)


def vmem(n):
    return [pl.BlockSpec(memory_space=pltpu.VMEM)] * n


def shards_block(acts, pre_act, emb_grad, filters):
    rows, c_in = acts.shape
    wide = filters.shape[1]
    unit = c_in // 8
    total = 8 * rows
    h, zl, y, x, c = coords()
    q = 2 * zl + y
    at = jnp.stack([h, zl, y, x, c]).astype(jnp.int32)
    scale = 1.0 / math.sqrt(total)
    part = functools.partial(lax.dynamic_index_in_dim, axis=0, keepdims=False)

    dz = dz_block(pre_act, emb_grad)
    blocks = [dz] + [along_seq(dz, lambda i, s=s: (i + 2 * s) % 8) for s in (1, 2, 3)]
    pairs = []
    for block in blocks:
        pairs += [block, along_seq(block, lambda i: i ^ 1)]

    own = [filters[m * unit : (m + 1) * unit] for m in range(5)]
    weights = [own[0]] + [in_half(own[m], m) for m in (1, 2, 3)] + [own[4]]

    mine = lax.dynamic_slice_in_dim(acts, 2 * unit * (2 * x + c), 2 * unit, axis=1)
    halves = jnp.stack([mine[:, :unit], mine[:, unit:]])
    got = jnp.stack([send(part(halves, y ^ b), turn(a, b)) for a in range(2) for b in range(2)])
    other = send(got, SWAP_X)
    far, far_other = send(got, SWAP_C), send(other, SWAP_C)
    left = pl.pallas_call(
        functools.partial(left_kernel, rows, unit),
        out_shape=jax.ShapeDtypeStruct((5, unit, total), BF16),
        in_specs=[pl.BlockSpec(memory_space=pltpu.SMEM)] + vmem(4),
        out_specs=vmem(1)[0],
        scratch_shapes=[pltpu.VMEM((2, unit, total), F32)],
        compiler_params=pltpu.CompilerParams(vmem_limit_bytes=48 << 20),
        cost_estimate=pl.CostEstimate(flops=0, bytes_accessed=6 << 20, transcendentals=0),
        name="left",
    )(at, got, other, far, far_other)

    partial, dz_all = pl.pallas_call(
        functools.partial(input_kernel, rows, unit),
        out_shape=(
            jax.ShapeDtypeStruct((2, 2, 4, rows, unit), BF16),
            jax.ShapeDtypeStruct((total, wide), BF16),
        ),
        in_specs=[pl.BlockSpec(memory_space=pltpu.SMEM)] + vmem(13),
        out_specs=tuple(vmem(2)),
        scratch_shapes=[pltpu.VMEM((5, unit, wide), BF16), pltpu.VMEM((5, total + 16, unit), F32)],
        compiler_params=pltpu.CompilerParams(vmem_limit_bytes=48 << 20),
        cost_estimate=pl.CostEstimate(flops=2 * total * 5 * unit * wide, bytes_accessed=6 << 20, transcendentals=0),
        name="input",
    )(at, *pairs, *weights)

    summed = partial[0].astype(F32) + send(partial[1], SWAP_C).astype(F32)
    crossed = send(part(summed, 1 - x).astype(BF16), SWAP_X)
    ready = (part(summed, x) + crossed.astype(F32)).astype(BF16)
    units = []
    for b in range(2):
        came = [send(part(ready, 2 * (h ^ a) + (y ^ b)), turn(a, b)).astype(F32) for a in range(2)]
        units.append((came[0] + came[1]).astype(BF16))
    input_grad = jnp.where(y == 0, jnp.concatenate(units, axis=1), jnp.concatenate(units[::-1], axis=1))

    grads = jnp.dot(left.reshape(5 * unit, total), dz_all, preferred_element_type=F32).reshape(5, unit, wide) * scale
    pieces = [part(grads, q)]
    for m in (1, 2, 3):
        pieces.append(in_half(part(grads, (q + 5 - m) % 5).astype(BF16), -m).astype(F32))
    pieces.append(part(grads, q + 1))
    return input_grad, jnp.concatenate(pieces, axis=0)


def solution(mesh):
    in_specs = (P("seq", None), P("seq", "section"), P("seq", "section"), P("seq", "section"))
    out_specs = (P("seq", "section"), P("seq", "section"))
    block = mesh.shape["seq"] == 8 and mesh.shape["section"] == 4
    body = shards_block if block else shards_any
    return jax.shard_map(body, mesh=mesh, in_specs=in_specs, out_specs=out_specs, check_vma=False)
```

```python
import functools
import math

import jax
import jax.numpy as jnp
from jax import lax
from jax.experimental import pallas as pl
from jax.experimental.pallas import tpu as pltpu
from jax.sharding import PartitionSpec as P

KERNEL = 5
SEQS = 1
F32 = jnp.float32
BF16 = jnp.bfloat16


def with_halo(shard, sides, width):
    for axis, dim in sides:
        size, length = (lax.axis_size(axis), shard.shape[dim])
        up = [(i, (i + 1) % size) for i in range(size - 1)]
        down = [(j, i) for i, j in up]
        last = lax.slice_in_dim(shard, length - width, length, axis=dim)
        first = lax.slice_in_dim(shard, 0, width, axis=dim)
        before = lax.ppermute(last, axis, up)
        after = lax.ppermute(first, axis, down)
        shard = jnp.concatenate([before, shard, after], axis=dim)
    return shard


def gelu_slope(value):
    cumul = 0.5 * (1.0 + lax.erf(value * 0.7071067811865476))
    dens = jnp.exp(-0.5 * value * value) * 0.3989422804014327
    return cumul + value * dens


def dz_block(pre_act, emb_grad):
    upward = jnp.repeat(emb_grad.astype(F32), 2, axis=0) * 0.5
    return (upward * gelu_slope(pre_act.astype(F32))).astype(BF16)


def shards_any(acts, pre_act, emb_grad, filters):
    rows = acts.shape[0]
    c_in = acts.shape[1]
    dz_grad = dz_block(pre_act, emb_grad)
    total_rows = rows * lax.axis_size("seq")
    length = total_rows // SEQS
    first = lax.axis_index("seq") * rows
    positions = first - 2 + jnp.arange(rows + 4, dtype=jnp.int32)
    inside = (jnp.floor_divide(positions, length) == first // length).astype(BF16)[:, None]
    scale_value = 1.0 / math.sqrt(total_rows)
    grad_rim = with_halo(dz_grad, (("seq", 0),), 2) * inside
    whole_term = (
        jnp.concatenate(
            [
                jnp.einsum(
                    "rc,ro->co",
                    acts,
                    grad_rim[4 - k : 4 - k + rows],
                    preferred_element_type=F32,
                )
                for k in range(KERNEL)
            ],
            axis=0,
        )
        * scale_value
    )
    piece = lax.all_gather(filters, "seq", axis=0, tiled=True)
    width = piece.shape[0]
    product = jnp.einsum("ro,no->rn", grad_rim, piece, preferred_element_type=F32)
    tap_of = jnp.arange(width, dtype=jnp.int32) // c_in
    total = jnp.zeros((rows, width), F32)
    for k in range(KERNEL):
        total = total + jnp.where((tap_of == k)[None, :], product[4 - k : 4 - k + rows], 0.0)
    partial_input = total.reshape(rows, KERNEL, c_in).sum(axis=1)
    input_grad = lax.psum_scatter(partial_input, "section", scatter_dimension=1, tiled=True).astype(BF16)
    filter_grad = lax.psum_scatter(whole_term, "seq", scatter_dimension=0, tiled=True)
    return (input_grad, filter_grad)


TAPS = (((0, 0), (0, 1), (1, 0), (1, 1), (2, 0)), ((2, 0), (3, 1), (3, 0), (4, 1), (4, 0)))


def coords():
    i, j = lax.axis_index("seq"), lax.axis_index("section")
    return i // 4, (i // 2) % 2, i % 2, j // 2, j % 2


def send(value, place):
    pairs = []
    for g in range(32):
        h, zl, y, x, c = (g >> 4) & 1, (g >> 3) & 1, (g >> 2) & 1, (g >> 1) & 1, g & 1
        h, zl, y, x, c = place(h, zl, y, x, c)
        pairs.append((g, h * 16 + zl * 8 + y * 4 + x * 2 + c))
    return lax.ppermute(value, ("seq", "section"), pairs)


def in_half(value, step):
    return lax.ppermute(value, "seq", [(i, 4 * (i // 4) + (i % 4 + step) % 4) for i in range(8)])


SWAP_H = lambda h, zl, y, x, c: (1 - h, zl, y, x, c)
SWAP_Z = lambda h, zl, y, x, c: (h, 1 - zl, y, x, c)
SWAP_Y = lambda h, zl, y, x, c: (h, zl, 1 - y, x, c)
SWAP_X = lambda h, zl, y, x, c: (h, zl, y, 1 - x, c)
SWAP_C = lambda h, zl, y, x, c: (h, zl, y, x, 1 - c)


def turn(a, b):
    return lambda h, zl, y, x, c: (h ^ a, c, y ^ b, x, zl)


def dz_kernel(pre_ref, emb_ref, out_ref):
    rows, half = pre_ref.shape[0], emb_ref.shape[0]
    row = lax.broadcasted_iota(jnp.int32, (rows, half), 0)
    pair = lax.broadcasted_iota(jnp.int32, (rows, half), 1)
    twice = (row // 2 == pair).astype(BF16)
    up = jnp.dot(twice, emb_ref[...], preferred_element_type=F32) * 0.5
    out_ref[...] = (up * gelu_slope(pre_ref[...].astype(F32))).astype(BF16)


def units_kernel(unit, filters_ref, *out_refs):
    for m, ref in enumerate(out_refs):
        ref[...] = filters_ref[m * unit : (m + 1) * unit, :]


def cut_kernel(unit, acts_ref, *out_refs):
    _, _, y, x, c = coords()
    for j in range(4):

        @pl.when(2 * x + c == j)
        def _():
            for s in range(2):
                first = (2 * j + s) * unit
                value = acts_ref[:, first : first + unit].astype(F32).T.astype(BF16)
                for b, ref in enumerate(out_refs):

                    @pl.when(y ^ b == s)
                    def _():
                        ref[...] = value


def join_kernel(*refs):
    for n, ref in enumerate(refs[:-1]):
        refs[-1][n] = ref[...]


def input_kernel(rows, unit, *refs):
    dz_refs, w_refs, (keep_ref, away_ref, dz_ref) = refs[:8], refs[8:13], refs[13:16]
    weights, runs, arrived = refs[16:]
    h, zl, y, _, c = coords()
    q = 2 * zl + y
    copies = []
    for s in range(8):
        block = 4 * (h ^ (s // 4)) + 2 * (zl ^ ((s // 2) % 2)) + (y ^ (s % 2))
        there = dz_ref.at[pl.ds(pl.multiple_of(block * rows, rows), rows), :]
        copies.append(pltpu.make_async_copy(dz_refs[s], there, arrived.at[s]))
    for m in range(5):
        there = weights.at[pl.ds(pl.multiple_of(lax.rem(q + 5 - m, 5) * unit, 16), unit), :]
        copies.append(pltpu.make_async_copy(w_refs[m], there, arrived.at[8 + m]))
    for copy in copies:
        copy.start()
    for copy in copies:
        copy.wait()

    long = 2 * rows
    for r in range(4):
        run = runs.at[2 * (r // 2) + ((r % 2) ^ c)]
        lines = slice(max(r * long - 8, 0), min((r + 1) * long + 8, 4 * long))
        value = dz_ref[lines, :].astype(F32)
        if r == 0:
            value = jnp.concatenate([jnp.zeros((8, value.shape[1]), F32), value], axis=0)
        if r == 3:
            value = jnp.concatenate([value, jnp.zeros((8, value.shape[1]), F32)], axis=0)
        run[...] = value

    for half in range(2):

        @pl.when(h == half)
        def _():
            for t in range(8):
                sums = [None, None]
                for tap in range(2 * half, 2 * half + 3):
                    first = 8 + (t % 2) * rows + 2 - tap
                    shifted = runs[t // 2, first : first + rows, :].astype(BF16)
                    slots = [v for v in range(5) if TAPS[half][v][0] == tap]
                    term = lax.dot_general(
                        weights[slots[0] * unit : (slots[-1] + 1) * unit, :],
                        shifted,
                        (((1,), (1,)), ((), ())),
                        preferred_element_type=F32,
                    )
                    for n, v in enumerate(slots):
                        which = TAPS[half][v][1]
                        one = term[n * unit : (n + 1) * unit]
                        sums[which] = one if sums[which] is None else sums[which] + one
                for which in range(2):
                    ref = away_ref if (t // 2) % 2 else keep_ref
                    ref[which ^ half, 2 * (t // 4) + t % 2] = sums[which].astype(ref.dtype)


def cores_kernel(keep_ref, came_ref, keep_out, away_out):
    x = coords()[3]
    keep_out[...] = keep_ref[x] + came_ref[x].astype(F32)
    away_out[...] = (keep_ref[1 - x] + came_ref[1 - x].astype(F32)).astype(BF16)


def owners_kernel(keep_ref, came_ref, *out_refs):
    h, _, y, _, _ = coords()
    for n, ref in enumerate(out_refs):
        block = 2 * (h ^ (n // 2)) + (y ^ (n % 2))
        ref[...] = (keep_ref[block] + came_ref[block].astype(F32)).astype(BF16)


def last_kernel(unit, *refs):
    y, out_ref = coords()[2], refs[4]
    for b in range(2):
        first = pl.multiple_of((y ^ b) * unit, 16)
        out_ref[pl.ds(first, unit), :] = (refs[b][...].astype(F32) + refs[2 + b][...].astype(F32)).astype(BF16)


def left_kernel(rows, unit, s00, s10, s01, s11, out_ref, lines):
    h, _, y, x, c = coords()
    for xr, cr, ref in ((0, 0, s00), (1, 0, s10), (0, 1, s01), (1, 1, s11)):
        which = x ^ xr ^ h
        for a in range(2):
            for b in range(2):
                block = 4 * (h ^ a) + 2 * (c ^ cr) + (y ^ b)
                lines[which, :, pl.ds(pl.multiple_of(block * rows, rows), rows)] = ref[2 * a + b].astype(F32)
    total = 8 * rows
    place = lax.broadcasted_iota(jnp.int32, (unit, total), 1)
    for half in range(2):

        @pl.when(h == half)
        def _():
            for v, (tap, which) in enumerate(TAPS[half]):
                line = lines[which]
                if tap != 2:
                    line = pltpu.roll(line, (2 - tap) % total, 1)
                    fits = (place + (tap - 2) >= 0) & (place + (tap - 2) < total)
                    line = jnp.where(fits, line, 0.0)
                out_ref[v] = line.astype(BF16)


def filter_kernel(scale, left_ref, dz_ref, first_ref, s1_ref, s2_ref, s3_ref, last_ref):
    _, zl, y, _, _ = coords()
    for m, ref in enumerate((first_ref, s1_ref, s2_ref, s3_ref, last_ref)):
        slot = lax.rem(2 * zl + y + 5 - m, 5)
        grad = jnp.dot(left_ref[slot], dz_ref[...], preferred_element_type=F32) * scale
        ref[...] = grad.astype(ref.dtype)


def home_kernel(unit, first_ref, s1_ref, s2_ref, s3_ref, last_ref, out_ref):
    for m, ref in enumerate((first_ref, s1_ref, s2_ref, s3_ref, last_ref)):
        out_ref[m * unit : (m + 1) * unit, :] = ref[...].astype(F32)


def call(kernel, name, shapes, args, scratch=(), flops=0, mib=16, anywhere=False):
    many = isinstance(shapes, tuple)
    spec = pl.BlockSpec(memory_space=pltpu.VMEM)
    nbytes = sum(a.size * a.dtype.itemsize for a in args + (shapes if many else (shapes,)))
    return pl.pallas_call(
        kernel,
        out_shape=shapes,
        in_specs=[pl.BlockSpec(memory_space=pl.ANY) if anywhere else spec] * len(args),
        out_specs=(spec,) * len(shapes) if many else spec,
        scratch_shapes=list(scratch),
        compiler_params=pltpu.CompilerParams(vmem_limit_bytes=mib << 20),
        cost_estimate=pl.CostEstimate(flops=flops, bytes_accessed=nbytes, transcendentals=0),
        name=name,
    )(*args)


def shards_block(acts, pre_act, emb_grad, filters):
    rows, c_in = acts.shape
    wide = filters.shape[1]
    unit = c_in // 8
    total = 8 * rows
    flops = 2 * total * 5 * unit * wide
    shape = jax.ShapeDtypeStruct
    block, weight, pos = shape((rows, wide), BF16), shape((unit, wide), BF16), shape((unit, rows), BF16)

    tie = lax.optimization_barrier
    dz = call(dz_kernel, "dz", block, (pre_act, emb_grad), mib=8)
    own0, own1 = call(functools.partial(cut_kernel, unit), "cut", (pos, pos), (acts,), mib=8)
    dz_h, dz_z, dz_y = send(dz, SWAP_H), send(dz, SWAP_Z), send(dz, SWAP_Y)
    t11, t01 = send(own1, turn(1, 1)), send(own1, turn(0, 1))

    dz_h, dz_z, dz_y, t11, t01, own0, filters = tie((dz_h, dz_z, dz_y, t11, t01, own0, filters))
    dz_hz, dz_zy, dz_hy = send(dz_h, SWAP_Z), send(dz_z, SWAP_Y), send(dz_h, SWAP_Y)
    t10, t00 = send(own0, turn(1, 0)), send(own0, turn(0, 0))
    units = call(functools.partial(units_kernel, unit), "units", (weight,) * 5, (filters,), mib=4)

    dz_hz, dz_zy, dz_hy, t10, t00, *units = tie((dz_hz, dz_zy, dz_hy, t10, t00, *units))
    dz_hzy = send(dz_hz, SWAP_Y)
    weights = tuple(in_half(w, m) if m in (1, 2, 3) else w for m, w in enumerate(units))
    got = call(join_kernel, "join", shape((4, unit, rows), BF16), (t00, t01, t10, t11), mib=4)
    other = send(got, SWAP_X)

    dz_hzy, other, *weights = tie((dz_hzy, other, *weights))
    far, far_other = send(got, SWAP_C), send(other, SWAP_C)
    left = call(
        functools.partial(left_kernel, rows, unit),
        "left",
        shape((5, unit, total), BF16),
        (got, other, far, far_other),
        scratch=[pltpu.VMEM((2, unit, total), F32)],
    )
    blocks = (dz, dz_y, dz_z, dz_zy, dz_h, dz_hy, dz_hz, dz_hzy)

    keep, away, dz_all = call(
        functools.partial(input_kernel, rows, unit),
        "input",
        (shape((2, 4, unit, rows), F32), shape((2, 4, unit, rows), BF16), shape((total, wide), BF16)),
        blocks + tuple(weights),
        scratch=[
            pltpu.VMEM((5 * unit, wide), BF16),
            pltpu.VMEM((4, 2 * rows + 16, wide), F32),
            pltpu.SemaphoreType.DMA((13,)),
        ],
        flops=flops,
        anywhere=True,
    )

    keep, away = call(
        cores_kernel,
        "cores",
        (shape((4, unit, rows), F32), shape((4, unit, rows), BF16)),
        (keep, send(away, SWAP_C)),
    )
    ready = call(owners_kernel, "owners", (pos,) * 4, (keep, send(away, SWAP_X)))
    came = tuple(send(r, turn(n // 2, n % 2)) for n, r in enumerate(ready))
    input_grad = call(functools.partial(last_kernel, unit), "last", shape((2 * unit, rows), BF16), came, mib=4).T

    grads = call(
        functools.partial(filter_kernel, 1.0 / math.sqrt(total)),
        "filter",
        tuple(shape((unit, wide), F32 if m in (0, 4) else BF16) for m in range(5)),
        (left, dz_all),
        flops=flops,
    )
    grads = tuple(in_half(grad, -m) if m in (1, 2, 3) else grad for m, grad in enumerate(grads))
    filter_grad = call(functools.partial(home_kernel, unit), "home", shape((5 * unit, wide), F32), grads, mib=8)
    return input_grad, filter_grad


def solution(mesh):
    in_specs = (P("seq", None), P("seq", "section"), P("seq", "section"), P("seq", "section"))
    out_specs = (P("seq", "section"), P("seq", "section"))
    block = mesh.shape["seq"] == 8 and mesh.shape["section"] == 4
    body = shards_block if block else shards_any
    return jax.shard_map(body, mesh=mesh, in_specs=in_specs, out_specs=out_specs, check_vma=False)
```

```python
import functools
import math

import jax
import jax.numpy as jnp
from jax import lax
from jax.experimental import pallas as pl
from jax.experimental.pallas import tpu as pltpu
from jax.sharding import PartitionSpec as P

KERNEL = 5
SEQS = 1
F32 = jnp.float32
BF16 = jnp.bfloat16


def with_halo(shard, sides, width):
    for axis, dim in sides:
        size, length = (lax.axis_size(axis), shard.shape[dim])
        up = [(i, (i + 1) % size) for i in range(size - 1)]
        down = [(j, i) for i, j in up]
        last = lax.slice_in_dim(shard, length - width, length, axis=dim)
        first = lax.slice_in_dim(shard, 0, width, axis=dim)
        before = lax.ppermute(last, axis, up)
        after = lax.ppermute(first, axis, down)
        shard = jnp.concatenate([before, shard, after], axis=dim)
    return shard


def gelu_slope(value):
    cumul = 0.5 * (1.0 + lax.erf(value * 0.7071067811865476))
    dens = jnp.exp(-0.5 * value * value) * 0.3989422804014327
    return cumul + value * dens


def dz_block(pre_act, emb_grad):
    upward = jnp.repeat(emb_grad.astype(F32), 2, axis=0) * 0.5
    return (upward * gelu_slope(pre_act.astype(F32))).astype(BF16)


def shards_any(acts, pre_act, emb_grad, filters):
    rows = acts.shape[0]
    c_in = acts.shape[1]
    dz_grad = dz_block(pre_act, emb_grad)
    total_rows = rows * lax.axis_size("seq")
    length = total_rows // SEQS
    first = lax.axis_index("seq") * rows
    positions = first - 2 + jnp.arange(rows + 4, dtype=jnp.int32)
    inside = (jnp.floor_divide(positions, length) == first // length).astype(BF16)[:, None]
    scale_value = 1.0 / math.sqrt(total_rows)
    grad_rim = with_halo(dz_grad, (("seq", 0),), 2) * inside
    whole_term = (
        jnp.concatenate(
            [
                jnp.einsum(
                    "rc,ro->co",
                    acts,
                    grad_rim[4 - k : 4 - k + rows],
                    preferred_element_type=F32,
                )
                for k in range(KERNEL)
            ],
            axis=0,
        )
        * scale_value
    )
    piece = lax.all_gather(filters, "seq", axis=0, tiled=True)
    width = piece.shape[0]
    product = jnp.einsum("ro,no->rn", grad_rim, piece, preferred_element_type=F32)
    tap_of = jnp.arange(width, dtype=jnp.int32) // c_in
    total = jnp.zeros((rows, width), F32)
    for k in range(KERNEL):
        total = total + jnp.where((tap_of == k)[None, :], product[4 - k : 4 - k + rows], 0.0)
    partial_input = total.reshape(rows, KERNEL, c_in).sum(axis=1)
    input_grad = lax.psum_scatter(partial_input, "section", scatter_dimension=1, tiled=True).astype(BF16)
    filter_grad = lax.psum_scatter(whole_term, "seq", scatter_dimension=0, tiled=True)
    return (input_grad, filter_grad)


TAPS = (((0, 0), (0, 1), (1, 0), (1, 1), (2, 0)), ((2, 0), (3, 1), (3, 0), (4, 1), (4, 0)))


def coords():
    i, j = lax.axis_index("seq"), lax.axis_index("section")
    return i // 4, (i // 2) % 2, i % 2, j // 2, j % 2


def send(value, place):
    pairs = []
    for g in range(32):
        h, zl, y, x, c = (g >> 4) & 1, (g >> 3) & 1, (g >> 2) & 1, (g >> 1) & 1, g & 1
        h, zl, y, x, c = place(h, zl, y, x, c)
        pairs.append((g, h * 16 + zl * 8 + y * 4 + x * 2 + c))
    return lax.ppermute(value, ("seq", "section"), pairs)


def in_half(value, step):
    return lax.ppermute(value, "seq", [(i, 4 * (i // 4) + (i % 4 + step) % 4) for i in range(8)])


SWAP_H = lambda h, zl, y, x, c: (1 - h, zl, y, x, c)
SWAP_Z = lambda h, zl, y, x, c: (h, 1 - zl, y, x, c)
SWAP_Y = lambda h, zl, y, x, c: (h, zl, 1 - y, x, c)
SWAP_ZY = lambda h, zl, y, x, c: (h, 1 - zl, 1 - y, x, c)
SWAP_X = lambda h, zl, y, x, c: (h, zl, y, 1 - x, c)
SWAP_C = lambda h, zl, y, x, c: (h, zl, y, x, 1 - c)


def turn(a, b):
    return lambda h, zl, y, x, c: (h ^ a, c, y ^ b, x, zl)


def dz_kernel(pre_hbm, emb_hbm, filters_hbm, out_ref, along_ref, pre_ref, emb_ref, weight_ref, arrived):
    rows, unit = pre_ref.shape[0], weight_ref.shape[0]
    first = pl.multiple_of((1 + 2 * coords()[2]) * unit, 16)
    copies = [
        pltpu.make_async_copy(emb_hbm, emb_ref, arrived.at[0]),
        pltpu.make_async_copy(pre_hbm, pre_ref, arrived.at[1]),
        pltpu.make_async_copy(filters_hbm.at[pl.ds(first, unit), :], weight_ref, arrived.at[2]),
    ]
    for copy in copies:
        copy.start()
    half = emb_ref.shape[0]
    row = lax.broadcasted_iota(jnp.int32, (rows, half), 0)
    pair = lax.broadcasted_iota(jnp.int32, (rows, half), 1)
    twice = (row // 2 == pair).astype(BF16)
    for copy in copies:
        copy.wait()
    up = jnp.dot(twice, emb_ref[...], preferred_element_type=F32) * 0.5
    value = (up * gelu_slope(pre_ref[...].astype(F32))).astype(BF16)
    out_ref[...] = value
    along_ref[:rows] = value
    along_ref[rows:] = weight_ref[...]


def units_kernel(unit, filters_ref, first_ref, middle_ref, last_ref, across_ref):
    for m, ref in ((0, first_ref), (2, middle_ref), (4, last_ref)):
        ref[...] = filters_ref[m * unit : (m + 1) * unit, :]
    first = pl.multiple_of((3 - 2 * coords()[2]) * unit, 16)
    across_ref[...] = filters_ref[pl.ds(first, unit), :]


def cut_kernel(unit, acts_ref, *out_refs):
    _, _, y, x, c = coords()
    for j in range(4):

        @pl.when(2 * x + c == j)
        def _():
            for s in range(2):
                first = (2 * j + s) * unit
                value = acts_ref[:, first : first + unit].astype(F32).T.astype(BF16)
                for b, ref in enumerate(out_refs):

                    @pl.when(y ^ b == s)
                    def _():
                        ref[...] = value


def join_kernel(*refs):
    for n, ref in enumerate(refs[:-1]):
        refs[-1][n] = ref[...]


EDGE = 16


def place_dz(rows, ref, s):
    h, zl, y, _, _ = coords()
    block = 4 * (h ^ (s // 4)) + 2 * (zl ^ ((s // 2) % 2)) + (y ^ (s % 2))
    return ref.at[pl.ds(pl.multiple_of(block * rows + EDGE, EDGE), rows), :]


def gather_kernel(rows, *refs):
    out_ref = refs[-1]
    zeros = jnp.zeros((EDGE, out_ref.shape[1]), BF16)
    out_ref[:EDGE] = zeros
    out_ref[EDGE + 8 * rows :] = zeros
    for s, ref in enumerate(refs[:-1]):
        place_dz(rows, out_ref, s)[...] = ref[:rows]


def input_terms(rows, unit, dz_ref, weights, out_ref, side):
    h, _, _, _, c = coords()
    for half in range(2):

        @pl.when(h == half)
        def _():
            for n in range(4):
                first = (4 * (n // 2) + 2 * (c ^ side) + n % 2) * rows
                first = pl.multiple_of(first, EDGE)
                window = dz_ref[pl.ds(first, rows + 2 * EDGE), :]
                exact = window.astype(F32)
                sums = [None, None]
                for tap in range(2 * half, 2 * half + 3):
                    if tap == 2:
                        shifted = window[EDGE : EDGE + rows]
                    else:
                        shifted = exact[EDGE + 2 - tap : EDGE + 2 - tap + rows].astype(BF16)
                    slots = [v for v in range(5) if TAPS[half][v][0] == tap]
                    term = lax.dot_general(
                        weights[slots[0] * unit : (slots[-1] + 1) * unit, :],
                        shifted,
                        (((1,), (1,)), ((), ())),
                        preferred_element_type=F32,
                    )
                    for k, v in enumerate(slots):
                        which = TAPS[half][v][1]
                        one = term[k * unit : (k + 1) * unit]
                        sums[which] = one if sums[which] is None else sums[which] + one
                for which in range(2):
                    out_ref[(n // 2) ^ half, which ^ half, n % 2] = sums[which].astype(out_ref.dtype)


def away_kernel(rows, unit, most_ref, dz_last, *refs):
    w_refs, (dz_ref, weights, out_ref) = refs[:5], refs[5:]
    _, zl, y, _, _ = coords()
    place_dz(rows, dz_ref, 7)[...] = dz_last[...]
    for m, ref in zip((0, 2, 4, 1 + 2 * y, 3 - 2 * y), w_refs):
        slot = lax.rem(2 * zl + y + 5 - m, 5)
        first = ref.shape[0] - unit
        weights[pl.ds(pl.multiple_of(slot * unit, EDGE), unit), :] = ref[first:]
    input_terms(rows, unit, dz_ref, weights, out_ref, 1)


def keep_kernel(rows, unit, dz_ref, weights, out_ref):
    input_terms(rows, unit, dz_ref, weights, out_ref, 0)


def cores_kernel(a, keep_ref, came_ref, keep_out, away_out):
    x = coords()[3]
    keep_out[...] = keep_ref[a, x] + came_ref[a, x].astype(F32)
    away_out[...] = (keep_ref[a, 1 - x] + came_ref[a, 1 - x].astype(F32)).astype(BF16)


def owners_kernel(keep_ref, came_ref, *out_refs):
    y = coords()[2]
    for b, ref in enumerate(out_refs):
        ref[...] = (keep_ref[y ^ b] + came_ref[y ^ b].astype(F32)).astype(BF16)


def last_kernel(unit, *refs):
    y, out_ref = coords()[2], refs[4]
    for b in range(2):
        first = pl.multiple_of((y ^ b) * unit, 16)
        out_ref[pl.ds(first, unit), :] = (refs[b][...].astype(F32) + refs[2 + b][...].astype(F32)).astype(BF16)


def left_kernel(rows, unit, s00, s10, s01, s11, out_ref, lines):
    h, _, y, x, c = coords()
    for xr, cr, ref in ((0, 0, s00), (1, 0, s10), (0, 1, s01), (1, 1, s11)):
        which = x ^ xr ^ h
        for a in range(2):
            for b in range(2):
                block = 4 * (h ^ a) + 2 * (c ^ cr) + (y ^ b)
                lines[which, :, pl.ds(pl.multiple_of(block * rows, rows), rows)] = ref[2 * a + b].astype(F32)
    total = 8 * rows
    place = lax.broadcasted_iota(jnp.int32, (unit, total), 1)
    for half in range(2):

        @pl.when(h == half)
        def _():
            for v, (tap, which) in enumerate(TAPS[half]):
                line = lines[which]
                if tap != 2:
                    line = pltpu.roll(line, (2 - tap) % total, 1)
                    fits = (place + (tap - 2) >= 0) & (place + (tap - 2) < total)
                    line = jnp.where(fits, line, 0.0)
                out_ref[v] = line.astype(BF16)


def filter_kernel(scale, left_ref, dz_ref, first_ref, s1_ref, s2_ref, s3_ref, last_ref):
    _, zl, y, _, _ = coords()
    for m, ref in enumerate((first_ref, s1_ref, s2_ref, s3_ref, last_ref)):
        slot = lax.rem(2 * zl + y + 5 - m, 5)
        grad = jnp.dot(left_ref[slot], dz_ref[EDGE:-EDGE, :], preferred_element_type=F32) * scale
        ref[...] = grad.astype(ref.dtype)


def home_kernel(unit, first_ref, s1_ref, s2_ref, s3_ref, last_ref, out_ref):
    for m, ref in enumerate((first_ref, s1_ref, s2_ref, s3_ref, last_ref)):
        out_ref[m * unit : (m + 1) * unit, :] = ref[...].astype(F32)


def call(kernel, name, shapes, args, scratch=(), flops=0, mib=16, anywhere=False, alias={}):
    many = isinstance(shapes, tuple)
    spec = pl.BlockSpec(memory_space=pltpu.VMEM)
    nbytes = sum(a.size * a.dtype.itemsize for a in args + (shapes if many else (shapes,)))
    return pl.pallas_call(
        kernel,
        out_shape=shapes,
        in_specs=[pl.BlockSpec(memory_space=pl.ANY) if anywhere else spec] * len(args),
        out_specs=(spec,) * len(shapes) if many else spec,
        scratch_shapes=list(scratch),
        input_output_aliases=alias,
        compiler_params=pltpu.CompilerParams(vmem_limit_bytes=mib << 20),
        cost_estimate=pl.CostEstimate(flops=0, bytes_accessed=1024, transcendentals=0),
        name=name,
    )(*args)


def shards_block(acts, pre_act, emb_grad, filters):
    rows, c_in = acts.shape
    wide = filters.shape[1]
    unit = c_in // 8
    total = 8 * rows
    flops = 2 * total * 5 * unit * wide
    shape = jax.ShapeDtypeStruct
    block, weight, pos = shape((rows, wide), BF16), shape((unit, wide), BF16), shape((unit, rows), BF16)

    tie = lax.optimization_barrier
    dz, along = call(
        dz_kernel,
        "dz",
        (block, shape((rows + unit, wide), BF16)),
        (pre_act, emb_grad, filters),
        scratch=[
            pltpu.VMEM(pre_act.shape, BF16),
            pltpu.VMEM(emb_grad.shape, BF16),
            pltpu.VMEM((unit, wide), BF16),
            pltpu.SemaphoreType.DMA((3,)),
        ],
        mib=60,
        anywhere=True,
    )
    own0, own1 = call(functools.partial(cut_kernel, unit), "cut", (pos, pos), (acts,), mib=8)
    dz_h, dz_z, dz_y = send(dz, SWAP_H), send(dz, SWAP_Z), send(along, SWAP_Y)
    t11, t01 = send(own1, turn(1, 1)), send(own1, turn(0, 1))

    dz_zy = send(dz_z, SWAP_Y)
    dz_h, dz_y, t11, t01, own0, filters = tie((dz_h, dz_y, t11, t01, own0, filters))
    dz_hz, dz_hy = send(dz_h, SWAP_Z), send(dz_h, SWAP_Y)
    t10, t00 = send(own0, turn(1, 0)), send(own0, turn(0, 0))
    units = call(functools.partial(units_kernel, unit), "units", (weight,) * 4, (filters,), mib=4)

    dz_hz, dz_zy, dz_hy, t10, t00, *units = tie((dz_hz, dz_zy, dz_hy, t10, t00, *units))
    got = call(join_kernel, "join", shape((4, unit, rows), BF16), (t00, t01, t10, t11), mib=4)
    other = send(got, SWAP_X)
    dz_hzy = send(dz_hz, SWAP_Y)
    w0, w2, w4, wd = units
    w2, wd = send(w2, SWAP_Z), send(wd, SWAP_ZY)
    far = send(got, SWAP_C)

    weights = (w0, w2, w4, wd, dz_y)
    dz_hzy, other, far, *weights = tie((dz_hzy, other, far, *weights))
    far_other = send(other, SWAP_C)
    left = call(
        functools.partial(left_kernel, rows, unit),
        "left",
        shape((5, unit, total), BF16),
        (got, other, far, far_other),
        scratch=[pltpu.VMEM((2, unit, total), F32)],
    )
    padded = shape((total + 2 * EDGE, wide), BF16)
    most = call(
        functools.partial(gather_kernel, rows),
        "gather",
        padded,
        (dz, dz_y, dz_z, dz_zy, dz_h, dz_hy, dz_hz),
        mib=8,
    )
    dz_all, ordered, away = call(
        functools.partial(away_kernel, rows, unit),
        "away",
        (padded, shape((5 * unit, wide), BF16), shape((2, 2, 2, unit, rows), BF16)),
        (most, dz_hzy) + tuple(weights),
        flops=flops // 2,
        alias={0: 0},
    )
    keep = call(
        functools.partial(keep_kernel, rows, unit),
        "keep",
        shape((2, 2, 2, unit, rows), F32),
        (dz_all, ordered),
        flops=flops // 2,
    )

    came = send(away, SWAP_C)
    parts = (shape((2, unit, rows), F32), shape((2, unit, rows), BF16))
    keep_far, far = call(functools.partial(cores_kernel, 1), "cores_far", parts, (keep, came))
    keep, came, keep_far = tie((keep, came, keep_far))
    keep_near, near = call(functools.partial(cores_kernel, 0), "cores_near", parts, (keep, came))
    far, near = send(far, SWAP_X), send(near, SWAP_X)
    far_blocks = call(owners_kernel, "far", (pos,) * 2, (keep_far, far), mib=8)
    near_blocks = call(owners_kernel, "near", (pos,) * 2, (keep_near, near), mib=8)
    far_blocks = [send(block, turn(1, b)) for b, block in enumerate(far_blocks)]
    near_blocks = [send(block, turn(0, b)) for b, block in enumerate(near_blocks)]
    came = tuple(far_blocks + near_blocks)
    input_grad = call(functools.partial(last_kernel, unit), "last", shape((2 * unit, rows), BF16), came, mib=4).T

    grads = call(
        functools.partial(filter_kernel, 1.0 / math.sqrt(total)),
        "filter",
        tuple(shape((unit, wide), F32 if m in (0, 4) else BF16) for m in range(5)),
        (left, dz_all),
        flops=flops,
    )
    grads = tuple(in_half(grad, -m) if m in (1, 2, 3) else grad for m, grad in enumerate(grads))
    filter_grad = call(functools.partial(home_kernel, unit), "home", shape((5 * unit, wide), F32), grads, mib=8)
    return input_grad, filter_grad


def solution(mesh):
    in_specs = (P("seq", None), P("seq", "section"), P("seq", "section"), P("seq", "section"))
    out_specs = (P("seq", "section"), P("seq", "section"))
    block = mesh.shape["seq"] == 8 and mesh.shape["section"] == 4
    body = shards_block if block else shards_any
    return jax.shard_map(body, mesh=mesh, in_specs=in_specs, out_specs=out_specs, check_vma=False)
```

```python
import functools
import math

import jax
import jax.numpy as jnp
from jax import lax
from jax.experimental import pallas as pl
from jax.experimental.pallas import tpu as pltpu
from jax.sharding import PartitionSpec as P

KERNEL = 5
SEQS = 1
F32 = jnp.float32
BF16 = jnp.bfloat16


def with_halo(shard, sides, width):
    for axis, dim in sides:
        size, length = (lax.axis_size(axis), shard.shape[dim])
        up = [(i, (i + 1) % size) for i in range(size - 1)]
        down = [(j, i) for i, j in up]
        last = lax.slice_in_dim(shard, length - width, length, axis=dim)
        first = lax.slice_in_dim(shard, 0, width, axis=dim)
        before = lax.ppermute(last, axis, up)
        after = lax.ppermute(first, axis, down)
        shard = jnp.concatenate([before, shard, after], axis=dim)
    return shard


def gelu_slope(value):
    cumul = 0.5 * (1.0 + lax.erf(value * 0.7071067811865476))
    dens = jnp.exp(-0.5 * value * value) * 0.3989422804014327
    return cumul + value * dens


def dz_block(pre_act, emb_grad):
    upward = jnp.repeat(emb_grad.astype(F32), 2, axis=0) * 0.5
    return (upward * gelu_slope(pre_act.astype(F32))).astype(BF16)


def shards_any(acts, pre_act, emb_grad, filters):
    rows = acts.shape[0]
    c_in = acts.shape[1]
    dz_grad = dz_block(pre_act, emb_grad)
    total_rows = rows * lax.axis_size("seq")
    length = total_rows // SEQS
    first = lax.axis_index("seq") * rows
    positions = first - 2 + jnp.arange(rows + 4, dtype=jnp.int32)
    inside = (jnp.floor_divide(positions, length) == first // length).astype(BF16)[:, None]
    scale_value = 1.0 / math.sqrt(total_rows)
    grad_rim = with_halo(dz_grad, (("seq", 0),), 2) * inside
    whole_term = (
        jnp.concatenate(
            [
                jnp.einsum(
                    "rc,ro->co",
                    acts,
                    grad_rim[4 - k : 4 - k + rows],
                    preferred_element_type=F32,
                )
                for k in range(KERNEL)
            ],
            axis=0,
        )
        * scale_value
    )
    piece = lax.all_gather(filters, "seq", axis=0, tiled=True)
    width = piece.shape[0]
    product = jnp.einsum("ro,no->rn", grad_rim, piece, preferred_element_type=F32)
    tap_of = jnp.arange(width, dtype=jnp.int32) // c_in
    total = jnp.zeros((rows, width), F32)
    for k in range(KERNEL):
        total = total + jnp.where((tap_of == k)[None, :], product[4 - k : 4 - k + rows], 0.0)
    partial_input = total.reshape(rows, KERNEL, c_in).sum(axis=1)
    input_grad = lax.psum_scatter(partial_input, "section", scatter_dimension=1, tiled=True).astype(BF16)
    filter_grad = lax.psum_scatter(whole_term, "seq", scatter_dimension=0, tiled=True)
    return (input_grad, filter_grad)


TAPS = (((0, 0), (0, 1), (1, 0), (1, 1), (2, 0)), ((2, 0), (3, 1), (3, 0), (4, 1), (4, 0)))


def coords():
    i, j = lax.axis_index("seq"), lax.axis_index("section")
    return i // 4, (i // 2) % 2, i % 2, j // 2, j % 2


def send(value, place):
    pairs = []
    for g in range(32):
        h, zl, y, x, c = (g >> 4) & 1, (g >> 3) & 1, (g >> 2) & 1, (g >> 1) & 1, g & 1
        h, zl, y, x, c = place(h, zl, y, x, c)
        pairs.append((g, h * 16 + zl * 8 + y * 4 + x * 2 + c))
    return lax.ppermute(value, ("seq", "section"), pairs)


def in_half(value, step):
    return lax.ppermute(value, "seq", [(i, 4 * (i // 4) + (i % 4 + step) % 4) for i in range(8)])


SWAP_H = lambda h, zl, y, x, c: (1 - h, zl, y, x, c)
SWAP_Z = lambda h, zl, y, x, c: (h, 1 - zl, y, x, c)
SWAP_Y = lambda h, zl, y, x, c: (h, zl, 1 - y, x, c)
SWAP_ZY = lambda h, zl, y, x, c: (h, 1 - zl, 1 - y, x, c)
SWAP_X = lambda h, zl, y, x, c: (h, zl, y, 1 - x, c)
SWAP_C = lambda h, zl, y, x, c: (h, zl, y, x, 1 - c)


def turn(a, b):
    return lambda h, zl, y, x, c: (h ^ a, c, y ^ b, x, zl)


def dz_kernel(pre_hbm, emb_hbm, filters_hbm, out_ref, along_ref, pre_ref, emb_ref, weight_ref, arrived):
    rows, unit = pre_ref.shape[0], weight_ref.shape[0]
    first = pl.multiple_of((1 + 2 * coords()[2]) * unit, 16)
    copies = [
        pltpu.make_async_copy(emb_hbm, emb_ref, arrived.at[0]),
        pltpu.make_async_copy(pre_hbm, pre_ref, arrived.at[1]),
        pltpu.make_async_copy(filters_hbm.at[pl.ds(first, unit), :], weight_ref, arrived.at[2]),
    ]
    for copy in copies:
        copy.start()
    half = emb_ref.shape[0]
    row = lax.broadcasted_iota(jnp.int32, (rows, half), 0)
    pair = lax.broadcasted_iota(jnp.int32, (rows, half), 1)
    twice = (row // 2 == pair).astype(BF16)
    for copy in copies:
        copy.wait()
    up = jnp.dot(twice, emb_ref[...], preferred_element_type=F32) * 0.5
    value = (up * gelu_slope(pre_ref[...].astype(F32))).astype(BF16)
    out_ref[...] = value
    along_ref[:rows] = value
    along_ref[rows:] = weight_ref[...]


def units_kernel(unit, filters_ref, first_ref, middle_ref, last_ref, across_ref):
    for m, ref in ((0, first_ref), (2, middle_ref), (4, last_ref)):
        ref[...] = filters_ref[m * unit : (m + 1) * unit, :]
    first = pl.multiple_of((3 - 2 * coords()[2]) * unit, 16)
    across_ref[...] = filters_ref[pl.ds(first, unit), :]


def cut_kernel(unit, acts_ref, *out_refs):
    _, _, y, x, c = coords()
    for j in range(4):

        @pl.when(2 * x + c == j)
        def _():
            for s in range(2):
                first = (2 * j + s) * unit
                value = acts_ref[:, first : first + unit].astype(F32).T.astype(BF16)
                for b, ref in enumerate(out_refs):

                    @pl.when(y ^ b == s)
                    def _():
                        ref[...] = value


def join_kernel(*refs):
    for n, ref in enumerate(refs[:-1]):
        refs[-1][n] = ref[...]


EDGE = 16


def place_dz(rows, ref, s):
    h, zl, y, _, _ = coords()
    block = 4 * (h ^ (s // 4)) + 2 * (zl ^ ((s // 2) % 2)) + (y ^ (s % 2))
    return ref.at[pl.ds(pl.multiple_of(block * rows + EDGE, EDGE), rows), :]


def gather_kernel(rows, *refs):
    out_ref = refs[-1]
    zeros = jnp.zeros((EDGE, out_ref.shape[1]), BF16)
    out_ref[:EDGE] = zeros
    out_ref[EDGE + 8 * rows :] = zeros
    for s, ref in enumerate(refs[:-1]):
        place_dz(rows, out_ref, s)[...] = ref[:rows]


def input_terms(rows, unit, dz_ref, weights, out_ref, side):
    h, _, _, _, c = coords()
    for half in range(2):

        @pl.when(h == half)
        def _():
            for n in range(4):
                first = (4 * (n // 2) + 2 * (c ^ side) + n % 2) * rows
                first = pl.multiple_of(first, EDGE)
                window = dz_ref[pl.ds(first, rows + 2 * EDGE), :]
                exact = window.astype(F32)
                sums = [None, None]
                for tap in range(2 * half, 2 * half + 3):
                    if tap == 2:
                        shifted = window[EDGE : EDGE + rows]
                    else:
                        shifted = exact[EDGE + 2 - tap : EDGE + 2 - tap + rows].astype(BF16)
                    slots = [v for v in range(5) if TAPS[half][v][0] == tap]
                    term = lax.dot_general(
                        weights[slots[0] * unit : (slots[-1] + 1) * unit, :],
                        shifted,
                        (((1,), (1,)), ((), ())),
                        preferred_element_type=F32,
                    )
                    for k, v in enumerate(slots):
                        which = TAPS[half][v][1]
                        one = term[k * unit : (k + 1) * unit]
                        sums[which] = one if sums[which] is None else sums[which] + one
                for which in range(2):
                    out_ref[(n // 2) ^ half, which ^ half, n % 2] = sums[which].astype(out_ref.dtype)


def away_kernel(rows, unit, most_ref, dz_last, *refs):
    w_refs, (dz_ref, weights, out_ref) = refs[:5], refs[5:]
    _, zl, y, _, _ = coords()
    place_dz(rows, dz_ref, 7)[...] = dz_last[...]
    for m, ref in zip((0, 2, 4, 1 + 2 * y, 3 - 2 * y), w_refs):
        slot = lax.rem(2 * zl + y + 5 - m, 5)
        first = ref.shape[0] - unit
        weights[pl.ds(pl.multiple_of(slot * unit, EDGE), unit), :] = ref[first:]
    input_terms(rows, unit, dz_ref, weights, out_ref, 1)


def keep_kernel(rows, unit, dz_ref, weights, out_ref):
    input_terms(rows, unit, dz_ref, weights, out_ref, 0)


def cores_kernel(a, keep_ref, came_ref, keep_out, away_out):
    x = coords()[3]
    keep_out[...] = keep_ref[a, x] + came_ref[a, x].astype(F32)
    away_out[...] = (keep_ref[a, 1 - x] + came_ref[a, 1 - x].astype(F32)).astype(BF16)


def owners_kernel(keep_ref, came_ref, *out_refs):
    y = coords()[2]
    for b, ref in enumerate(out_refs):
        ref[...] = (keep_ref[y ^ b] + came_ref[y ^ b].astype(F32)).astype(BF16)


def last_kernel(unit, *refs):
    y, out_ref = coords()[2], refs[4]
    for b in range(2):
        first = pl.multiple_of((y ^ b) * unit, 16)
        out_ref[pl.ds(first, unit), :] = (refs[b][...].astype(F32) + refs[2 + b][...].astype(F32)).astype(BF16)


def left_kernel(rows, unit, s00, s10, s01, s11, out_ref, lines):
    h, _, y, x, c = coords()
    for xr, cr, ref in ((0, 0, s00), (1, 0, s10), (0, 1, s01), (1, 1, s11)):
        which = x ^ xr ^ h
        for a in range(2):
            for b in range(2):
                block = 4 * (h ^ a) + 2 * (c ^ cr) + (y ^ b)
                lines[which, :, pl.ds(pl.multiple_of(block * rows, rows), rows)] = ref[2 * a + b].astype(F32)
    total = 8 * rows
    place = lax.broadcasted_iota(jnp.int32, (unit, total), 1)
    for half in range(2):

        @pl.when(h == half)
        def _():
            for v, (tap, which) in enumerate(TAPS[half]):
                line = lines[which]
                if tap != 2:
                    line = pltpu.roll(line, (2 - tap) % total, 1)
                    fits = (place + (tap - 2) >= 0) & (place + (tap - 2) < total)
                    line = jnp.where(fits, line, 0.0)
                out_ref[v] = line.astype(BF16)


def filter_kernel(scale, left_ref, dz_ref, first_ref, s1_ref, s2_ref, s3_ref, last_ref):
    _, zl, y, _, _ = coords()
    for m, ref in enumerate((first_ref, s1_ref, s2_ref, s3_ref, last_ref)):
        slot = lax.rem(2 * zl + y + 5 - m, 5)
        grad = jnp.dot(left_ref[slot], dz_ref[EDGE:-EDGE, :], preferred_element_type=F32) * scale
        ref[...] = grad.astype(ref.dtype)


def home_kernel(unit, first_ref, s1_ref, s2_ref, s3_ref, last_ref, out_ref):
    for m, ref in enumerate((first_ref, s1_ref, s2_ref, s3_ref, last_ref)):
        out_ref[m * unit : (m + 1) * unit, :] = ref[...].astype(F32)


def call(kernel, name, shapes, args, scratch=(), flops=0, mib=16, anywhere=False, alias={}):
    many = isinstance(shapes, tuple)
    spec = pl.BlockSpec(memory_space=pltpu.VMEM)
    nbytes = sum(a.size * a.dtype.itemsize for a in args + (shapes if many else (shapes,)))
    return pl.pallas_call(
        kernel,
        out_shape=shapes,
        in_specs=[pl.BlockSpec(memory_space=pl.ANY) if anywhere else spec] * len(args),
        out_specs=(spec,) * len(shapes) if many else spec,
        scratch_shapes=list(scratch),
        input_output_aliases=alias,
        compiler_params=pltpu.CompilerParams(vmem_limit_bytes=mib << 20),
        cost_estimate=pl.CostEstimate(flops=0, bytes_accessed=1024, transcendentals=0),
        name=name,
    )(*args)


def shards_block(acts, pre_act, emb_grad, filters):
    rows, c_in = acts.shape
    wide = filters.shape[1]
    unit = c_in // 8
    total = 8 * rows
    flops = 2 * total * 5 * unit * wide
    shape = jax.ShapeDtypeStruct
    block, weight, pos = shape((rows, wide), BF16), shape((unit, wide), BF16), shape((unit, rows), BF16)

    tie = lax.optimization_barrier
    dz, along = call(
        dz_kernel,
        "dz",
        (block, shape((rows + unit, wide), BF16)),
        (pre_act, emb_grad, filters),
        scratch=[
            pltpu.VMEM(pre_act.shape, BF16),
            pltpu.VMEM(emb_grad.shape, BF16),
            pltpu.VMEM((unit, wide), BF16),
            pltpu.SemaphoreType.DMA((3,)),
        ],
        mib=60,
        anywhere=True,
    )
    own0, own1 = call(functools.partial(cut_kernel, unit), "cut", (pos, pos), (acts,), mib=8)
    dz_h, dz_z, dz_y = send(dz, SWAP_H), send(dz, SWAP_Z), send(along, SWAP_Y)
    w0, w2, w4, wd = call(functools.partial(units_kernel, unit), "units", (weight,) * 4, (filters,), mib=4)
    t01, t00 = send(own1, turn(0, 1)), send(own0, turn(0, 0))
    dz_zy = send(dz_z, SWAP_Y)
    near_got = call(join_kernel, "join_near", shape((2, unit, rows), BF16), (t00, t01), mib=4)
    far_got = send(near_got, SWAP_H)
    dz_h, dz_y, wd, w2 = tie((dz_h, dz_y, wd, w2))
    dz_hz, dz_hy = send(dz_h, SWAP_Z), send(dz_h, SWAP_Y)
    wd = send(wd, SWAP_ZY)

    dz_hz, dz_zy, dz_hy, wd, w2, far_got = tie((dz_hz, dz_zy, dz_hy, wd, w2, far_got))
    got = call(join_kernel, "join", shape((2, 2, unit, rows), BF16), (near_got, far_got), mib=4)
    got = got.reshape(4, unit, rows)
    other = send(got, SWAP_X)
    dz_hzy = send(dz_hz, SWAP_Y)
    w2 = send(w2, SWAP_Z)
    far = send(got, SWAP_C)

    weights = (w0, w2, w4, wd, dz_y)
    dz_hzy, other, far, *weights = tie((dz_hzy, other, far, *weights))
    far_other = send(other, SWAP_C)
    left = call(
        functools.partial(left_kernel, rows, unit),
        "left",
        shape((5, unit, total), BF16),
        (got, other, far, far_other),
        scratch=[pltpu.VMEM((2, unit, total), F32)],
    )
    padded = shape((total + 2 * EDGE, wide), BF16)
    most = call(
        functools.partial(gather_kernel, rows),
        "gather",
        padded,
        (dz, dz_y, dz_z, dz_zy, dz_h, dz_hy, dz_hz),
        mib=8,
    )
    dz_all, ordered, away = call(
        functools.partial(away_kernel, rows, unit),
        "away",
        (padded, shape((5 * unit, wide), BF16), shape((2, 2, 2, unit, rows), BF16)),
        (most, dz_hzy) + tuple(weights),
        flops=flops // 2,
        alias={0: 0},
    )
    keep = call(
        functools.partial(keep_kernel, rows, unit),
        "keep",
        shape((2, 2, 2, unit, rows), F32),
        (dz_all, ordered),
        flops=flops // 2,
    )

    came = send(away, SWAP_C)
    parts = (shape((2, unit, rows), F32), shape((2, unit, rows), BF16))
    keep_far, far = call(functools.partial(cores_kernel, 1), "cores_far", parts, (keep, came))
    keep, came, keep_far = tie((keep, came, keep_far))
    keep_near, near = call(functools.partial(cores_kernel, 0), "cores_near", parts, (keep, came))
    far, near = send(far, SWAP_X), send(near, SWAP_X)
    far_blocks = call(owners_kernel, "far", (pos,) * 2, (keep_far, far), mib=8)
    near_blocks = call(owners_kernel, "near", (pos,) * 2, (keep_near, near), mib=8)
    far_blocks = [send(block, turn(1, b)) for b, block in enumerate(far_blocks)]
    near_blocks = [send(block, turn(0, b)) for b, block in enumerate(near_blocks)]
    came = tuple(far_blocks + near_blocks)
    input_grad = call(functools.partial(last_kernel, unit), "last", shape((2 * unit, rows), BF16), came, mib=4).T

    grads = call(
        functools.partial(filter_kernel, 1.0 / math.sqrt(total)),
        "filter",
        tuple(shape((unit, wide), F32 if m in (0, 4) else BF16) for m in range(5)),
        (left, dz_all),
        flops=flops,
    )
    grads = tuple(in_half(grad, -m) if m in (1, 2, 3) else grad for m, grad in enumerate(grads))
    filter_grad = call(functools.partial(home_kernel, unit), "home", shape((5 * unit, wide), F32), grads, mib=8)
    return input_grad, filter_grad


def solution(mesh):
    in_specs = (P("seq", None), P("seq", "section"), P("seq", "section"), P("seq", "section"))
    out_specs = (P("seq", "section"), P("seq", "section"))
    block = mesh.shape["seq"] == 8 and mesh.shape["section"] == 4
    body = shards_block if block else shards_any
    return jax.shard_map(body, mesh=mesh, in_specs=in_specs, out_specs=out_specs, check_vma=False)
```

```python
import functools
import math

import jax
import jax.numpy as jnp
from jax import lax
from jax.experimental import pallas as pl
from jax.experimental.pallas import tpu as pltpu
from jax.sharding import PartitionSpec as P

KERNEL = 5
SEQS = 1
F32 = jnp.float32
BF16 = jnp.bfloat16


def with_halo(shard, sides, width):
    for axis, dim in sides:
        size, length = (lax.axis_size(axis), shard.shape[dim])
        up = [(i, (i + 1) % size) for i in range(size - 1)]
        down = [(j, i) for i, j in up]
        last = lax.slice_in_dim(shard, length - width, length, axis=dim)
        first = lax.slice_in_dim(shard, 0, width, axis=dim)
        before = lax.ppermute(last, axis, up)
        after = lax.ppermute(first, axis, down)
        shard = jnp.concatenate([before, shard, after], axis=dim)
    return shard


def gelu_slope(value):
    cumul = 0.5 * (1.0 + lax.erf(value * 0.7071067811865476))
    dens = jnp.exp(-0.5 * value * value) * 0.3989422804014327
    return cumul + value * dens


def dz_block(pre_act, emb_grad):
    upward = jnp.repeat(emb_grad.astype(F32), 2, axis=0) * 0.5
    return (upward * gelu_slope(pre_act.astype(F32))).astype(BF16)


def shards_any(acts, pre_act, emb_grad, filters):
    rows = acts.shape[0]
    c_in = acts.shape[1]
    dz_grad = dz_block(pre_act, emb_grad)
    total_rows = rows * lax.axis_size("seq")
    length = total_rows // SEQS
    first = lax.axis_index("seq") * rows
    positions = first - 2 + jnp.arange(rows + 4, dtype=jnp.int32)
    inside = (jnp.floor_divide(positions, length) == first // length).astype(BF16)[:, None]
    scale_value = 1.0 / math.sqrt(total_rows)
    grad_rim = with_halo(dz_grad, (("seq", 0),), 2) * inside
    whole_term = (
        jnp.concatenate(
            [
                jnp.einsum(
                    "rc,ro->co",
                    acts,
                    grad_rim[4 - k : 4 - k + rows],
                    preferred_element_type=F32,
                )
                for k in range(KERNEL)
            ],
            axis=0,
        )
        * scale_value
    )
    piece = lax.all_gather(filters, "seq", axis=0, tiled=True)
    width = piece.shape[0]
    product = jnp.einsum("ro,no->rn", grad_rim, piece, preferred_element_type=F32)
    tap_of = jnp.arange(width, dtype=jnp.int32) // c_in
    total = jnp.zeros((rows, width), F32)
    for k in range(KERNEL):
        total = total + jnp.where((tap_of == k)[None, :], product[4 - k : 4 - k + rows], 0.0)
    partial_input = total.reshape(rows, KERNEL, c_in).sum(axis=1)
    input_grad = lax.psum_scatter(partial_input, "section", scatter_dimension=1, tiled=True).astype(BF16)
    filter_grad = lax.psum_scatter(whole_term, "seq", scatter_dimension=0, tiled=True)
    return (input_grad, filter_grad)


TAPS = (((0, 0), (0, 1), (1, 0), (1, 1), (2, 0)), ((2, 0), (3, 1), (3, 0), (4, 1), (4, 0)))


def coords():
    i, j = lax.axis_index("seq"), lax.axis_index("section")
    return i // 4, (i // 2) % 2, i % 2, j // 2, j % 2


def send(value, place):
    pairs = []
    for g in range(32):
        h, zl, y, x, c = (g >> 4) & 1, (g >> 3) & 1, (g >> 2) & 1, (g >> 1) & 1, g & 1
        h, zl, y, x, c = place(h, zl, y, x, c)
        pairs.append((g, h * 16 + zl * 8 + y * 4 + x * 2 + c))
    return lax.ppermute(value, ("seq", "section"), pairs)


def in_half(value, step):
    return lax.ppermute(value, "seq", [(i, 4 * (i // 4) + (i % 4 + step) % 4) for i in range(8)])


SWAP_H = lambda h, zl, y, x, c: (1 - h, zl, y, x, c)
SWAP_Z = lambda h, zl, y, x, c: (h, 1 - zl, y, x, c)
SWAP_Y = lambda h, zl, y, x, c: (h, zl, 1 - y, x, c)
SWAP_X = lambda h, zl, y, x, c: (h, zl, y, 1 - x, c)
SWAP_C = lambda h, zl, y, x, c: (h, zl, y, x, 1 - c)


def turn(a, b):
    return lambda h, zl, y, x, c: (h ^ a, c, y ^ b, x, zl)


def dz_kernel(pre_hbm, emb_hbm, filters_hbm, out_ref, along_ref, pre_ref, emb_ref, weight_ref, arrived):
    rows, unit = pre_ref.shape[0], weight_ref.shape[1]
    y = coords()[2]
    copies = [
        pltpu.make_async_copy(emb_hbm, emb_ref, arrived.at[0]),
        pltpu.make_async_copy(pre_hbm, pre_ref, arrived.at[1]),
    ]
    for n, m in enumerate((1 + 2 * y, 3 - 2 * y)):
        first = pl.multiple_of(m * unit, 16)
        copies.append(
            pltpu.make_async_copy(filters_hbm.at[pl.ds(first, unit), :], weight_ref.at[n], arrived.at[2 + n])
        )
    for copy in copies:
        copy.start()
    half = emb_ref.shape[0]
    row = lax.broadcasted_iota(jnp.int32, (rows, half), 0)
    pair = lax.broadcasted_iota(jnp.int32, (rows, half), 1)
    twice = (row // 2 == pair).astype(BF16)
    for copy in copies:
        copy.wait()
    up = jnp.dot(twice, emb_ref[...], preferred_element_type=F32) * 0.5
    value = (up * gelu_slope(pre_ref[...].astype(F32))).astype(BF16)
    out_ref[...] = value
    along_ref[:rows] = value
    for n in range(2):
        along_ref[rows + n * unit : rows + (n + 1) * unit] = weight_ref[n]


def units_kernel(unit, filters_ref, came_ref, first_ref, last_ref, along_ref):
    first_ref[...] = filters_ref[:unit, :]
    last_ref[...] = filters_ref[4 * unit :, :]
    along_ref[:unit] = filters_ref[2 * unit : 3 * unit, :]
    along_ref[unit:] = came_ref[came_ref.shape[0] - unit :, :]


def cut_kernel(unit, acts_ref, *out_refs):
    _, _, y, x, c = coords()
    for j in range(4):

        @pl.when(2 * x + c == j)
        def _():
            for s in range(2):
                first = (2 * j + s) * unit
                value = acts_ref[:, first : first + unit].astype(F32).T.astype(BF16)
                for b, ref in enumerate(out_refs):

                    @pl.when(y ^ b == s)
                    def _():
                        ref[...] = value


def join_kernel(*refs):
    for n, ref in enumerate(refs[:-1]):
        refs[-1][n] = ref[...]


def pair_kernel(first_ref, last_ref, out_ref):
    half = first_ref.shape[0]
    out_ref[:half] = first_ref[...]
    out_ref[half:] = last_ref[...]


EDGE = 16


def place_dz(rows, ref, s):
    h, zl, y, _, _ = coords()
    block = 4 * (h ^ (s // 4)) + 2 * (zl ^ ((s // 2) % 2)) + (y ^ (s % 2))
    return ref.at[pl.ds(pl.multiple_of(block * rows + EDGE, EDGE), rows), :]


def gather_kernel(rows, *refs):
    out_ref = refs[-1]
    zeros = jnp.zeros((EDGE, out_ref.shape[1]), BF16)
    out_ref[:EDGE] = zeros
    out_ref[EDGE + 8 * rows :] = zeros
    for s, ref in enumerate(refs[:-1]):
        place_dz(rows, out_ref, s)[...] = ref[:rows]


def input_terms(rows, unit, dz_ref, weights, out_ref, side):
    h, _, _, _, c = coords()
    for half in range(2):

        @pl.when(h == half)
        def _():
            for n in range(4):
                first = (4 * (n // 2) + 2 * (c ^ side) + n % 2) * rows
                first = pl.multiple_of(first, EDGE)
                window = dz_ref[pl.ds(first, rows + 2 * EDGE), :]
                exact = window.astype(F32)
                sums = [None, None]
                for tap in range(2 * half, 2 * half + 3):
                    if tap == 2:
                        shifted = window[EDGE : EDGE + rows]
                    else:
                        shifted = exact[EDGE + 2 - tap : EDGE + 2 - tap + rows].astype(BF16)
                    slots = [v for v in range(5) if TAPS[half][v][0] == tap]
                    term = lax.dot_general(
                        weights[slots[0] * unit : (slots[-1] + 1) * unit, :],
                        shifted,
                        (((1,), (1,)), ((), ())),
                        preferred_element_type=F32,
                    )
                    for k, v in enumerate(slots):
                        which = TAPS[half][v][1]
                        one = term[k * unit : (k + 1) * unit]
                        sums[which] = one if sums[which] is None else sums[which] + one
                for which in range(2):
                    out_ref[(n // 2) ^ half, which ^ half, n % 2] = sums[which].astype(out_ref.dtype)


def away_kernel(rows, unit, most_ref, dz_last, *refs):
    first, last, along_z, along_y, dz_ref, weights, out_ref = refs
    _, zl, y, _, _ = coords()
    place_dz(rows, dz_ref, 7)[...] = dz_last[...]
    units = (
        (0, first, 0),
        (4, last, 0),
        (2, along_z, 0),
        (1 + 2 * y, along_z, unit),
        (3 - 2 * y, along_y, rows),
    )
    for m, ref, start in units:
        slot = lax.rem(2 * zl + y + 5 - m, 5)
        weights[pl.ds(pl.multiple_of(slot * unit, EDGE), unit), :] = ref[start : start + unit]
    input_terms(rows, unit, dz_ref, weights, out_ref, 1)


def keep_kernel(rows, unit, dz_ref, weights, out_ref):
    input_terms(rows, unit, dz_ref, weights, out_ref, 0)


def cores_kernel(a, keep_ref, came_ref, keep_out, away_out):
    x = coords()[3]
    keep_out[...] = keep_ref[a, x] + came_ref[a, x].astype(F32)
    away_out[...] = (keep_ref[a, 1 - x] + came_ref[a, 1 - x].astype(F32)).astype(BF16)


def owners_kernel(keep_ref, came_ref, *out_refs):
    y = coords()[2]
    for b, ref in enumerate(out_refs):
        ref[...] = (keep_ref[y ^ b] + came_ref[y ^ b].astype(F32)).astype(BF16)


def last_kernel(unit, *refs):
    y, out_ref = coords()[2], refs[4]
    for b in range(2):
        first = pl.multiple_of((y ^ b) * unit, 16)
        out_ref[pl.ds(first, unit), :] = (refs[b][...].astype(F32) + refs[2 + b][...].astype(F32)).astype(BF16)


def left_kernel(rows, unit, own_ref, came_ref, out_ref, lines):
    h, _, y, x, c = coords()
    for cr, ref in enumerate((own_ref, came_ref)):
        for n in range(8):
            which = x ^ (n // 4) ^ h
            block = 4 * (h ^ (n // 2 % 2)) + 2 * (c ^ cr) + (y ^ (n % 2))
            lines[which, :, pl.ds(pl.multiple_of(block * rows, rows), rows)] = ref[n].astype(F32)
    total = 8 * rows
    place = lax.broadcasted_iota(jnp.int32, (unit, total), 1)
    for half in range(2):

        @pl.when(h == half)
        def _():
            for v, (tap, which) in enumerate(TAPS[half]):
                line = lines[which]
                if tap != 2:
                    line = pltpu.roll(line, (2 - tap) % total, 1)
                    fits = (place + (tap - 2) >= 0) & (place + (tap - 2) < total)
                    line = jnp.where(fits, line, 0.0)
                out_ref[v] = line.astype(BF16)


def filter_kernel(scale, left_ref, dz_ref, first_ref, s1_ref, s2_ref, s3_ref, last_ref):
    _, zl, y, _, _ = coords()
    for m, ref in enumerate((first_ref, s1_ref, s2_ref, s3_ref, last_ref)):
        slot = lax.rem(2 * zl + y + 5 - m, 5)
        grad = jnp.dot(left_ref[slot], dz_ref[EDGE:-EDGE, :], preferred_element_type=F32) * scale
        ref[...] = grad.astype(ref.dtype)


def home_kernel(unit, first_ref, s1_ref, s2_ref, s3_ref, last_ref, out_ref):
    for m, ref in enumerate((first_ref, s1_ref, s2_ref, s3_ref, last_ref)):
        out_ref[m * unit : (m + 1) * unit, :] = ref[...].astype(F32)


def call(kernel, name, shapes, args, scratch=(), flops=0, mib=16, anywhere=False, alias={}):
    many = isinstance(shapes, tuple)
    spec = pl.BlockSpec(memory_space=pltpu.VMEM)
    nbytes = sum(a.size * a.dtype.itemsize for a in args + (shapes if many else (shapes,)))
    return pl.pallas_call(
        kernel,
        out_shape=shapes,
        in_specs=[pl.BlockSpec(memory_space=pl.ANY) if anywhere else spec] * len(args),
        out_specs=(spec,) * len(shapes) if many else spec,
        scratch_shapes=list(scratch),
        input_output_aliases=alias,
        compiler_params=pltpu.CompilerParams(vmem_limit_bytes=mib << 20),
        cost_estimate=pl.CostEstimate(flops=0, bytes_accessed=1024, transcendentals=0),
        name=name,
    )(*args)


def shards_block(acts, pre_act, emb_grad, filters):
    rows, c_in = acts.shape
    wide = filters.shape[1]
    unit = c_in // 8
    total = 8 * rows
    flops = 2 * total * 5 * unit * wide
    shape = jax.ShapeDtypeStruct
    block, weight, pos = shape((rows, wide), BF16), shape((unit, wide), BF16), shape((unit, rows), BF16)

    tie = lax.optimization_barrier
    dz, along = call(
        dz_kernel,
        "dz",
        (block, shape((rows + 2 * unit, wide), BF16)),
        (pre_act, emb_grad, filters),
        scratch=[
            pltpu.VMEM(pre_act.shape, BF16),
            pltpu.VMEM(emb_grad.shape, BF16),
            pltpu.VMEM((2, unit, wide), BF16),
            pltpu.SemaphoreType.DMA((4,)),
        ],
        mib=60,
        anywhere=True,
    )
    own0, own1 = call(functools.partial(cut_kernel, unit), "cut", (pos, pos), (acts,), mib=8)
    dz_h, dz_z, dz_y = send(dz, SWAP_H), send(dz, SWAP_Z), send(along, SWAP_Y)
    t01, t00 = send(own1, turn(0, 1)), send(own0, turn(0, 0))
    dz_zy = send(dz_z, SWAP_Y)
    near_got = call(join_kernel, "join_near", shape((2, unit, rows), BF16), (t00, t01), mib=4)
    far_got = send(near_got, SWAP_H)
    dz_h, dz_y, filters = tie((dz_h, dz_y, filters))
    dz_hz, dz_hy = send(dz_h, SWAP_Z), send(dz_h, SWAP_Y)

    w0, w4, along = call(
        functools.partial(units_kernel, unit),
        "units",
        (weight, weight, shape((2 * unit, wide), BF16)),
        (filters, dz_y),
        mib=4,
    )
    dz_hz, dz_zy, dz_hy, along, far_got = tie((dz_hz, dz_zy, dz_hy, along, far_got))
    got = call(join_kernel, "join", shape((2, 2, unit, rows), BF16), (near_got, far_got), mib=4)
    got = got.reshape(4, unit, rows)
    other = send(got, SWAP_X)
    dz_hzy = send(dz_hz, SWAP_Y)
    along = send(along, SWAP_Z)

    weights = (w0, w4, along, dz_y)
    dz_hzy, other, *weights = tie((dz_hzy, other, *weights))
    both = call(pair_kernel, "pair", shape((8, unit, rows), BF16), (got, other), mib=8)
    left = call(
        functools.partial(left_kernel, rows, unit),
        "left",
        shape((5, unit, total), BF16),
        (both, send(both, SWAP_C)),
        scratch=[pltpu.VMEM((2, unit, total), F32)],
    )
    padded = shape((total + 2 * EDGE, wide), BF16)
    most = call(
        functools.partial(gather_kernel, rows),
        "gather",
        padded,
        (dz, dz_y, dz_z, dz_zy, dz_h, dz_hy, dz_hz),
        mib=8,
    )
    dz_all, ordered, away = call(
        functools.partial(away_kernel, rows, unit),
        "away",
        (padded, shape((5 * unit, wide), BF16), shape((2, 2, 2, unit, rows), BF16)),
        (most, dz_hzy) + tuple(weights),
        flops=flops // 2,
        alias={0: 0},
    )
    keep = call(
        functools.partial(keep_kernel, rows, unit),
        "keep",
        shape((2, 2, 2, unit, rows), F32),
        (dz_all, ordered),
        flops=flops // 2,
    )

    came = send(away, SWAP_C)
    parts = (shape((2, unit, rows), F32), shape((2, unit, rows), BF16))
    keep_far, far = call(functools.partial(cores_kernel, 1), "cores_far", parts, (keep, came))
    keep, came, keep_far = tie((keep, came, keep_far))
    keep_near, near = call(functools.partial(cores_kernel, 0), "cores_near", parts, (keep, came))
    far, near = send(far, SWAP_X), send(near, SWAP_X)
    far_blocks = call(owners_kernel, "far", (pos,) * 2, (keep_far, far), mib=8)
    near_blocks = call(owners_kernel, "near", (pos,) * 2, (keep_near, near), mib=8)
    far_blocks = [send(block, turn(1, b)) for b, block in enumerate(far_blocks)]
    near_blocks = [send(block, turn(0, b)) for b, block in enumerate(near_blocks)]
    came = tuple(far_blocks + near_blocks)
    input_grad = call(functools.partial(last_kernel, unit), "last", shape((2 * unit, rows), BF16), came, mib=4).T

    grads = call(
        functools.partial(filter_kernel, 1.0 / math.sqrt(total)),
        "filter",
        tuple(shape((unit, wide), F32 if m in (0, 4) else BF16) for m in range(5)),
        (left, dz_all),
        flops=flops,
    )
    grads = tuple(in_half(grad, -m) if m in (1, 2, 3) else grad for m, grad in enumerate(grads))
    filter_grad = call(functools.partial(home_kernel, unit), "home", shape((5 * unit, wide), F32), grads, mib=8)
    return input_grad, filter_grad


def solution(mesh):
    in_specs = (P("seq", None), P("seq", "section"), P("seq", "section"), P("seq", "section"))
    out_specs = (P("seq", "section"), P("seq", "section"))
    block = mesh.shape["seq"] == 8 and mesh.shape["section"] == 4
    body = shards_block if block else shards_any
    return jax.shard_map(body, mesh=mesh, in_specs=in_specs, out_specs=out_specs, check_vma=False)
```

```python
import functools
import math

import jax
import jax.numpy as jnp
from jax import lax
from jax.experimental import pallas as pl
from jax.experimental.pallas import tpu as pltpu
from jax.sharding import PartitionSpec as P

KERNEL = 5
SEQS = 1
F32 = jnp.float32
BF16 = jnp.bfloat16


def with_halo(shard, sides, width):
    for axis, dim in sides:
        size, length = (lax.axis_size(axis), shard.shape[dim])
        up = [(i, (i + 1) % size) for i in range(size - 1)]
        down = [(j, i) for i, j in up]
        last = lax.slice_in_dim(shard, length - width, length, axis=dim)
        first = lax.slice_in_dim(shard, 0, width, axis=dim)
        before = lax.ppermute(last, axis, up)
        after = lax.ppermute(first, axis, down)
        shard = jnp.concatenate([before, shard, after], axis=dim)
    return shard


def gelu_slope(value):
    cumul = 0.5 * (1.0 + lax.erf(value * 0.7071067811865476))
    dens = jnp.exp(-0.5 * value * value) * 0.3989422804014327
    return cumul + value * dens


def dz_block(pre_act, emb_grad):
    upward = jnp.repeat(emb_grad.astype(F32), 2, axis=0) * 0.5
    return (upward * gelu_slope(pre_act.astype(F32))).astype(BF16)


def shards_any(acts, pre_act, emb_grad, filters):
    rows = acts.shape[0]
    c_in = acts.shape[1]
    dz_grad = dz_block(pre_act, emb_grad)
    total_rows = rows * lax.axis_size("seq")
    length = total_rows // SEQS
    first = lax.axis_index("seq") * rows
    positions = first - 2 + jnp.arange(rows + 4, dtype=jnp.int32)
    inside = (jnp.floor_divide(positions, length) == first // length).astype(BF16)[:, None]
    scale_value = 1.0 / math.sqrt(total_rows)
    grad_rim = with_halo(dz_grad, (("seq", 0),), 2) * inside
    whole_term = (
        jnp.concatenate(
            [
                jnp.einsum(
                    "rc,ro->co",
                    acts,
                    grad_rim[4 - k : 4 - k + rows],
                    preferred_element_type=F32,
                )
                for k in range(KERNEL)
            ],
            axis=0,
        )
        * scale_value
    )
    piece = lax.all_gather(filters, "seq", axis=0, tiled=True)
    width = piece.shape[0]
    product = jnp.einsum("ro,no->rn", grad_rim, piece, preferred_element_type=F32)
    tap_of = jnp.arange(width, dtype=jnp.int32) // c_in
    total = jnp.zeros((rows, width), F32)
    for k in range(KERNEL):
        total = total + jnp.where((tap_of == k)[None, :], product[4 - k : 4 - k + rows], 0.0)
    partial_input = total.reshape(rows, KERNEL, c_in).sum(axis=1)
    input_grad = lax.psum_scatter(partial_input, "section", scatter_dimension=1, tiled=True).astype(BF16)
    filter_grad = lax.psum_scatter(whole_term, "seq", scatter_dimension=0, tiled=True)
    return (input_grad, filter_grad)


TAPS = (((0, 0), (0, 1), (1, 0), (1, 1), (2, 0)), ((2, 0), (3, 1), (3, 0), (4, 1), (4, 0)))


def coords():
    i, j = lax.axis_index("seq"), lax.axis_index("section")
    return i // 4, (i // 2) % 2, i % 2, j // 2, j % 2


def send(value, place):
    pairs = []
    for g in range(32):
        h, zl, y, x, c = (g >> 4) & 1, (g >> 3) & 1, (g >> 2) & 1, (g >> 1) & 1, g & 1
        h, zl, y, x, c = place(h, zl, y, x, c)
        pairs.append((g, h * 16 + zl * 8 + y * 4 + x * 2 + c))
    return lax.ppermute(value, ("seq", "section"), pairs)


SWAP_H = lambda h, zl, y, x, c: (1 - h, zl, y, x, c)
SWAP_Z = lambda h, zl, y, x, c: (h, 1 - zl, y, x, c)
SWAP_Y = lambda h, zl, y, x, c: (h, zl, 1 - y, x, c)
SWAP_ZY = lambda h, zl, y, x, c: (h, 1 - zl, 1 - y, x, c)
SWAP_X = lambda h, zl, y, x, c: (h, zl, y, 1 - x, c)
SWAP_C = lambda h, zl, y, x, c: (h, zl, y, x, 1 - c)


def turn(a, b):
    return lambda h, zl, y, x, c: (h ^ a, c, y ^ b, x, zl)


def dz_kernel(pre_hbm, emb_hbm, filters_hbm, out_ref, along_ref, pre_ref, emb_ref, weight_ref, arrived):
    rows, unit = pre_ref.shape[0], weight_ref.shape[1]
    y = coords()[2]
    copies = [
        pltpu.make_async_copy(emb_hbm, emb_ref, arrived.at[0]),
        pltpu.make_async_copy(pre_hbm, pre_ref, arrived.at[1]),
    ]
    for n, m in enumerate((1 + 2 * y, 3 - 2 * y)):
        first = pl.multiple_of(m * unit, 16)
        copies.append(
            pltpu.make_async_copy(filters_hbm.at[pl.ds(first, unit), :], weight_ref.at[n], arrived.at[2 + n])
        )
    for copy in copies:
        copy.start()
    half = emb_ref.shape[0]
    row = lax.broadcasted_iota(jnp.int32, (rows, half), 0)
    pair = lax.broadcasted_iota(jnp.int32, (rows, half), 1)
    twice = (row // 2 == pair).astype(BF16)
    for copy in copies:
        copy.wait()
    up = jnp.dot(twice, emb_ref[...], preferred_element_type=F32) * 0.5
    value = (up * gelu_slope(pre_ref[...].astype(F32))).astype(BF16)
    out_ref[...] = value
    along_ref[:rows] = value
    for n in range(2):
        along_ref[rows + n * unit : rows + (n + 1) * unit] = weight_ref[n]


def units_kernel(unit, filters_ref, came_ref, first_ref, last_ref, along_ref):
    first_ref[...] = filters_ref[:unit, :]
    last_ref[...] = filters_ref[4 * unit :, :]
    along_ref[:unit] = filters_ref[2 * unit : 3 * unit, :]
    along_ref[unit:] = came_ref[came_ref.shape[0] - unit :, :]


def cut_kernel(unit, acts_ref, *out_refs):
    _, _, y, x, c = coords()
    for j in range(4):

        @pl.when(2 * x + c == j)
        def _():
            for s in range(2):
                first = (2 * j + s) * unit
                value = acts_ref[:, first : first + unit].astype(F32).T.astype(BF16)
                for b, ref in enumerate(out_refs):

                    @pl.when(y ^ b == s)
                    def _():
                        ref[...] = value


def join_kernel(*refs):
    for n, ref in enumerate(refs[:-1]):
        refs[-1][n] = ref[...]


def pair_kernel(first_ref, last_ref, out_ref):
    half = first_ref.shape[0]
    out_ref[:half] = first_ref[...]
    out_ref[half:] = last_ref[...]


EDGE = 16


def place_dz(rows, ref, s):
    h, zl, y, _, _ = coords()
    block = 4 * (h ^ (s // 4)) + 2 * (zl ^ ((s // 2) % 2)) + (y ^ (s % 2))
    return ref.at[pl.ds(pl.multiple_of(block * rows + EDGE, EDGE), rows), :]


def gather_kernel(rows, *refs):
    out_ref = refs[-1]
    zeros = jnp.zeros((EDGE, out_ref.shape[1]), BF16)
    out_ref[:EDGE] = zeros
    out_ref[EDGE + 8 * rows :] = zeros
    for s, ref in enumerate(refs[:-1]):
        place_dz(rows, out_ref, s)[...] = ref[:rows]


def input_terms(rows, unit, dz_ref, weights, out_ref, side):
    h, _, _, _, c = coords()
    for half in range(2):

        @pl.when(h == half)
        def _():
            for n in range(4):
                first = (4 * (n // 2) + 2 * (c ^ side) + n % 2) * rows
                first = pl.multiple_of(first, EDGE)
                window = dz_ref[pl.ds(first, rows + 2 * EDGE), :]
                exact = window.astype(F32)
                sums = [None, None]
                for tap in range(2 * half, 2 * half + 3):
                    if tap == 2:
                        shifted = window[EDGE : EDGE + rows]
                    else:
                        shifted = exact[EDGE + 2 - tap : EDGE + 2 - tap + rows].astype(BF16)
                    slots = [v for v in range(5) if TAPS[half][v][0] == tap]
                    term = lax.dot_general(
                        weights[slots[0] * unit : (slots[-1] + 1) * unit, :],
                        shifted,
                        (((1,), (1,)), ((), ())),
                        preferred_element_type=F32,
                    )
                    for k, v in enumerate(slots):
                        which = TAPS[half][v][1]
                        one = term[k * unit : (k + 1) * unit]
                        sums[which] = one if sums[which] is None else sums[which] + one
                for which in range(2):
                    out_ref[(n // 2) ^ half, which ^ half, n % 2] = sums[which].astype(out_ref.dtype)


def away_kernel(rows, unit, most_ref, dz_last, *refs):
    first, last, along_z, along_y, dz_ref, weights, out_ref = refs
    _, zl, y, _, _ = coords()
    place_dz(rows, dz_ref, 7)[...] = dz_last[...]
    units = (
        (0, first, 0),
        (4, last, 0),
        (2, along_z, 0),
        (1 + 2 * y, along_z, unit),
        (3 - 2 * y, along_y, rows),
    )
    for m, ref, start in units:
        slot = lax.rem(2 * zl + y + 5 - m, 5)
        weights[pl.ds(pl.multiple_of(slot * unit, EDGE), unit), :] = ref[start : start + unit]
    input_terms(rows, unit, dz_ref, weights, out_ref, 1)


def keep_kernel(rows, unit, dz_ref, weights, out_ref):
    input_terms(rows, unit, dz_ref, weights, out_ref, 0)


def cores_kernel(a, keep_ref, came_ref, keep_out, away_out):
    x = coords()[3]
    keep_out[...] = keep_ref[a, x] + came_ref[a, x].astype(F32)
    away_out[...] = (keep_ref[a, 1 - x] + came_ref[a, 1 - x].astype(F32)).astype(BF16)


def owners_kernel(keep_ref, came_ref, *out_refs):
    y = coords()[2]
    for b, ref in enumerate(out_refs):
        ref[...] = (keep_ref[y ^ b] + came_ref[y ^ b].astype(F32)).astype(BF16)


def last_kernel(unit, *refs):
    y, out_ref = coords()[2], refs[4]
    for b in range(2):
        first = pl.multiple_of((y ^ b) * unit, 16)
        out_ref[pl.ds(first, unit), :] = (refs[1 - b][...].astype(F32) + refs[3 - b][...].astype(F32)).astype(BF16)


def filter_kernel(scale, rows, own_ref, came_ref, dz_ref, first_ref, s1_ref, s2_ref, s3_ref, last_ref, lines, grads):
    h, zl, y, x, c = coords()
    unit, total = first_ref.shape[0], 8 * rows
    for cr, ref in enumerate((own_ref, came_ref)):
        for n in range(8):
            which = x ^ (n // 4) ^ h
            block = 4 * (h ^ (n // 2 % 2)) + 2 * (c ^ cr) + (y ^ (n % 2))
            lines[which, :, pl.ds(pl.multiple_of(block * rows, rows), rows)] = ref[n].astype(F32)
    lines[:, :, total:] = jnp.zeros((2, unit, lines.shape[2] - total), F32)
    for half in range(2):

        @pl.when(h == half)
        def _():
            for v, (tap, which) in enumerate(TAPS[half]):
                line = lines[which]
                if tap != 2:
                    line = pltpu.roll(line, (2 - tap) % lines.shape[2], 1)
                left = line[:, :total].astype(BF16)
                grads[v] = jnp.dot(left, dz_ref[EDGE:-EDGE, :], preferred_element_type=F32) * scale

    units = (0, 3 - 2 * y, 2, 1 + 2 * y, 4)
    for m, ref in zip(units, (first_ref, s1_ref, s2_ref, s3_ref, last_ref)):
        ref[...] = grads[lax.rem(2 * zl + y + 5 - m, 5)].astype(ref.dtype)


def home_kernel(unit, first_ref, zy_ref, z_ref, y_ref, last_ref, out_ref):
    y = coords()[2]
    for m, ref in ((0, first_ref), (1 + 2 * y, y_ref), (2, z_ref), (3 - 2 * y, zy_ref), (4, last_ref)):
        out_ref[pl.ds(pl.multiple_of(m * unit, 16), unit), :] = ref[...].astype(F32)


def call(kernel, name, shapes, args, scratch=(), flops=0, mib=16, anywhere=False, alias={}):
    many = isinstance(shapes, tuple)
    spec = pl.BlockSpec(memory_space=pltpu.VMEM)
    nbytes = sum(a.size * a.dtype.itemsize for a in args + (shapes if many else (shapes,)))
    return pl.pallas_call(
        kernel,
        out_shape=shapes,
        in_specs=[pl.BlockSpec(memory_space=pl.ANY) if anywhere else spec] * len(args),
        out_specs=(spec,) * len(shapes) if many else spec,
        scratch_shapes=list(scratch),
        input_output_aliases=alias,
        compiler_params=pltpu.CompilerParams(vmem_limit_bytes=mib << 20),
        cost_estimate=pl.CostEstimate(flops=0, bytes_accessed=1024, transcendentals=0),
        name=name,
    )(*args)


def shards_block(acts, pre_act, emb_grad, filters):
    rows, c_in = acts.shape
    wide = filters.shape[1]
    unit = c_in // 8
    total = 8 * rows
    flops = 2 * total * 5 * unit * wide
    shape = jax.ShapeDtypeStruct
    block, weight, pos = shape((rows, wide), BF16), shape((unit, wide), BF16), shape((unit, rows), BF16)

    tie = lax.optimization_barrier
    dz, along = call(
        dz_kernel,
        "dz",
        (block, shape((rows + 2 * unit, wide), BF16)),
        (pre_act, emb_grad, filters),
        scratch=[
            pltpu.VMEM(pre_act.shape, BF16),
            pltpu.VMEM(emb_grad.shape, BF16),
            pltpu.VMEM((2, unit, wide), BF16),
            pltpu.SemaphoreType.DMA((4,)),
        ],
        mib=60,
        anywhere=True,
    )
    own0, own1 = call(functools.partial(cut_kernel, unit), "cut", (pos, pos), (acts,), mib=8)
    dz_h, dz_z, dz_y = send(dz, SWAP_H), send(dz, SWAP_Z), send(along, SWAP_Y)
    t01, t00 = send(own1, turn(0, 1)), send(own0, turn(0, 0))
    dz_zy = send(dz_z, SWAP_Y)
    near_got = call(join_kernel, "join_near", shape((2, unit, rows), BF16), (t00, t01), mib=4)
    far_got = send(near_got, SWAP_H)
    dz_h, dz_y, filters = tie((dz_h, dz_y, filters))
    dz_hz, dz_hy = send(dz_h, SWAP_Z), send(dz_h, SWAP_Y)

    w0, w4, along = call(
        functools.partial(units_kernel, unit),
        "units",
        (weight, weight, shape((2 * unit, wide), BF16)),
        (filters, dz_y),
        mib=4,
    )
    dz_hz, dz_zy, dz_hy, along, far_got = tie((dz_hz, dz_zy, dz_hy, along, far_got))
    got = call(join_kernel, "join", shape((2, 2, unit, rows), BF16), (near_got, far_got), mib=4)
    got = got.reshape(4, unit, rows)
    other = send(got, SWAP_X)
    dz_hzy = send(dz_hz, SWAP_Y)
    along = send(along, SWAP_Z)

    weights = (w0, w4, along, dz_y)
    dz_hzy, other, *weights = tie((dz_hzy, other, *weights))
    both = call(pair_kernel, "pair", shape((8, unit, rows), BF16), (got, other), mib=8)
    far_both = send(both, SWAP_C)
    padded = shape((total + 2 * EDGE, wide), BF16)
    most = call(
        functools.partial(gather_kernel, rows),
        "gather",
        padded,
        (dz, dz_y, dz_z, dz_zy, dz_h, dz_hy, dz_hz),
        mib=8,
    )
    dz_all, ordered, away = call(
        functools.partial(away_kernel, rows, unit),
        "away",
        (padded, shape((5 * unit, wide), BF16), shape((2, 2, 2, unit, rows), BF16)),
        (most, dz_hzy) + tuple(weights),
        flops=flops // 2,
        alias={0: 0},
    )
    keep = call(
        functools.partial(keep_kernel, rows, unit),
        "keep",
        shape((2, 2, 2, unit, rows), F32),
        (dz_all, ordered),
        flops=flops // 2,
    )

    came = send(away, SWAP_C)
    parts = (shape((2, unit, rows), F32), shape((2, unit, rows), BF16))
    keep_far, far = call(functools.partial(cores_kernel, 1), "cores_far", parts, (keep, came))
    keep, came, keep_far = tie((keep, came, keep_far))
    keep_near, near = call(functools.partial(cores_kernel, 0), "cores_near", parts, (keep, came))
    far, near = send(far, SWAP_X), send(near, SWAP_X)
    far_blocks = call(owners_kernel, "far", (pos,) * 2, (keep_far, far), mib=8)
    near_blocks = call(owners_kernel, "near", (pos,) * 2, (keep_near, near), mib=8)
    far_blocks = [send(block, turn(1, b)) for b, block in enumerate(far_blocks)]
    near_blocks = [send(block, turn(0, b)) for b, block in enumerate(near_blocks)]
    came = tuple(far_blocks[::-1] + near_blocks[::-1])
    input_grad = call(functools.partial(last_kernel, unit), "last", shape((2 * unit, rows), BF16), came, mib=4).T

    grads = call(
        functools.partial(filter_kernel, 1.0 / math.sqrt(total), rows),
        "filter",
        tuple(shape((unit, wide), F32 if m in (0, 4) else BF16) for m in range(5)),
        (both, far_both, dz_all),
        scratch=[pltpu.VMEM((2, unit, total + 128), F32), pltpu.VMEM((5, unit, wide), F32)],
        flops=flops,
    )
    first, along_y, along_z, across, last = grads
    grads = (first, send(across, SWAP_ZY), send(along_z, SWAP_Z), send(along_y, SWAP_Y), last)
    filter_grad = call(functools.partial(home_kernel, unit), "home", shape((5 * unit, wide), F32), grads, mib=8)
    return input_grad, filter_grad


def solution(mesh):
    in_specs = (P("seq", None), P("seq", "section"), P("seq", "section"), P("seq", "section"))
    out_specs = (P("seq", "section"), P("seq", "section"))
    block = mesh.shape["seq"] == 8 and mesh.shape["section"] == 4
    body = shards_block if block else shards_any
    return jax.shard_map(body, mesh=mesh, in_specs=in_specs, out_specs=out_specs, check_vma=False)
```

```python
import functools
import math

import jax
import jax.numpy as jnp
from jax import lax
from jax.experimental import pallas as pl
from jax.experimental.pallas import tpu as pltpu
from jax.sharding import PartitionSpec as P

KERNEL = 5
SEQS = 1
F32 = jnp.float32
BF16 = jnp.bfloat16


def with_halo(shard, sides, width):
    for axis, dim in sides:
        size, length = (lax.axis_size(axis), shard.shape[dim])
        up = [(i, (i + 1) % size) for i in range(size - 1)]
        down = [(j, i) for i, j in up]
        last = lax.slice_in_dim(shard, length - width, length, axis=dim)
        first = lax.slice_in_dim(shard, 0, width, axis=dim)
        before = lax.ppermute(last, axis, up)
        after = lax.ppermute(first, axis, down)
        shard = jnp.concatenate([before, shard, after], axis=dim)
    return shard


def gelu_slope(value):
    cumul = 0.5 * (1.0 + lax.erf(value * 0.7071067811865476))
    dens = jnp.exp(-0.5 * value * value) * 0.3989422804014327
    return cumul + value * dens


def dz_block(pre_act, emb_grad):
    upward = jnp.repeat(emb_grad.astype(F32), 2, axis=0) * 0.5
    return (upward * gelu_slope(pre_act.astype(F32))).astype(BF16)


def shards_any(acts, pre_act, emb_grad, filters):
    rows = acts.shape[0]
    c_in = acts.shape[1]
    dz_grad = dz_block(pre_act, emb_grad)
    total_rows = rows * lax.axis_size("seq")
    length = total_rows // SEQS
    first = lax.axis_index("seq") * rows
    positions = first - 2 + jnp.arange(rows + 4, dtype=jnp.int32)
    inside = (jnp.floor_divide(positions, length) == first // length).astype(BF16)[:, None]
    scale_value = 1.0 / math.sqrt(total_rows)
    grad_rim = with_halo(dz_grad, (("seq", 0),), 2) * inside
    whole_term = (
        jnp.concatenate(
            [
                jnp.einsum(
                    "rc,ro->co",
                    acts,
                    grad_rim[4 - k : 4 - k + rows],
                    preferred_element_type=F32,
                )
                for k in range(KERNEL)
            ],
            axis=0,
        )
        * scale_value
    )
    piece = lax.all_gather(filters, "seq", axis=0, tiled=True)
    width = piece.shape[0]
    product = jnp.einsum("ro,no->rn", grad_rim, piece, preferred_element_type=F32)
    tap_of = jnp.arange(width, dtype=jnp.int32) // c_in
    total = jnp.zeros((rows, width), F32)
    for k in range(KERNEL):
        total = total + jnp.where((tap_of == k)[None, :], product[4 - k : 4 - k + rows], 0.0)
    partial_input = total.reshape(rows, KERNEL, c_in).sum(axis=1)
    input_grad = lax.psum_scatter(partial_input, "section", scatter_dimension=1, tiled=True).astype(BF16)
    filter_grad = lax.psum_scatter(whole_term, "seq", scatter_dimension=0, tiled=True)
    return (input_grad, filter_grad)


TAPS = (((0, 0), (0, 1), (1, 0), (1, 1), (2, 0)), ((2, 0), (3, 1), (3, 0), (4, 1), (4, 0)))


def coords():
    i, j = lax.axis_index("seq"), lax.axis_index("section")
    return i // 4, (i // 2) % 2, i % 2, j // 2, j % 2


def send(value, place):
    pairs = []
    for g in range(32):
        h, zl, y, x, c = (g >> 4) & 1, (g >> 3) & 1, (g >> 2) & 1, (g >> 1) & 1, g & 1
        h, zl, y, x, c = place(h, zl, y, x, c)
        pairs.append((g, h * 16 + zl * 8 + y * 4 + x * 2 + c))
    return lax.ppermute(value, ("seq", "section"), pairs)


SWAP_H = lambda h, zl, y, x, c: (1 - h, zl, y, x, c)
SWAP_Z = lambda h, zl, y, x, c: (h, 1 - zl, y, x, c)
SWAP_Y = lambda h, zl, y, x, c: (h, zl, 1 - y, x, c)
SWAP_ZY = lambda h, zl, y, x, c: (h, 1 - zl, 1 - y, x, c)
SWAP_X = lambda h, zl, y, x, c: (h, zl, y, 1 - x, c)
SWAP_C = lambda h, zl, y, x, c: (h, zl, y, x, 1 - c)


def turn(a, b):
    return lambda h, zl, y, x, c: (h ^ a, c, y ^ b, x, zl)


def dz_kernel(pre_hbm, emb_hbm, filters_hbm, out_ref, along_ref, pre_ref, emb_ref, weight_ref, arrived):
    rows, unit = pre_ref.shape[0], weight_ref.shape[1]
    y = coords()[2]
    copies = [
        pltpu.make_async_copy(emb_hbm, emb_ref, arrived.at[0]),
        pltpu.make_async_copy(pre_hbm, pre_ref, arrived.at[1]),
    ]
    for n, m in enumerate((1 + 2 * y, 3 - 2 * y)):
        first = pl.multiple_of(m * unit, 16)
        copies.append(
            pltpu.make_async_copy(filters_hbm.at[pl.ds(first, unit), :], weight_ref.at[n], arrived.at[2 + n])
        )
    for copy in copies:
        copy.start()
    half = emb_ref.shape[0]
    row = lax.broadcasted_iota(jnp.int32, (rows, half), 0)
    pair = lax.broadcasted_iota(jnp.int32, (rows, half), 1)
    twice = (row // 2 == pair).astype(BF16)
    for copy in copies[:2]:
        copy.wait()
    up = jnp.dot(twice, emb_ref[...], preferred_element_type=F32) * 0.5
    value = (up * gelu_slope(pre_ref[...].astype(F32))).astype(BF16)
    out_ref[...] = value
    along_ref[:rows] = value
    for copy in copies[2:]:
        copy.wait()
    for n in range(2):
        along_ref[rows + n * unit : rows + (n + 1) * unit] = weight_ref[n]


def units_kernel(unit, filters_ref, came_ref, first_ref, last_ref, along_ref):
    first_ref[...] = filters_ref[:unit, :]
    last_ref[...] = filters_ref[4 * unit :, :]
    along_ref[:unit] = filters_ref[2 * unit : 3 * unit, :]
    along_ref[unit:] = came_ref[came_ref.shape[0] - unit :, :]


def cut_kernel(unit, acts_hbm, *refs):
    out_refs, (acts_ref, arrived) = refs[:2], refs[2:]
    _, _, y, x, c = coords()
    for j in range(4):

        @pl.when(2 * x + c == j)
        def _():
            first = 2 * j * unit // 128 * 128
            last = min(first + acts_ref.shape[1], acts_hbm.shape[1])
            there = acts_ref.at[:, : last - first]
            copy = pltpu.make_async_copy(acts_hbm.at[:, first:last], there, arrived)
            copy.start()
            copy.wait()
            for s in range(2):
                start = (2 * j + s) * unit - first
                value = acts_ref[:, start : start + unit].astype(F32).T.astype(BF16)
                for b, ref in enumerate(out_refs):

                    @pl.when(y ^ b == s)
                    def _():
                        ref[...] = value


def join_kernel(*refs):
    for n, ref in enumerate(refs[:-1]):
        refs[-1][n] = ref[...]


def pair_kernel(first_ref, last_ref, out_ref):
    half = first_ref.shape[0]
    out_ref[:half] = first_ref[...]
    out_ref[half:] = last_ref[...]


EDGE = 16


def place_dz(rows, ref, s):
    h, zl, y, _, _ = coords()
    block = 4 * (h ^ (s // 4)) + 2 * (zl ^ ((s // 2) % 2)) + (y ^ (s % 2))
    return ref.at[pl.ds(pl.multiple_of(block * rows + EDGE, EDGE), rows), :]


def gather_kernel(rows, *refs):
    out_ref = refs[-1]
    zeros = jnp.zeros((EDGE, out_ref.shape[1]), BF16)
    out_ref[:EDGE] = zeros
    out_ref[EDGE + 8 * rows :] = zeros
    for s, ref in enumerate(refs[:-1]):
        place_dz(rows, out_ref, s)[...] = ref[:rows]


def input_terms(rows, unit, dz_ref, weights, out_ref, side):
    h, _, _, _, c = coords()
    for half in range(2):

        @pl.when(h == half)
        def _():
            for n in range(4):
                first = (4 * (n // 2) + 2 * (c ^ side) + n % 2) * rows
                first = pl.multiple_of(first, EDGE)
                window = dz_ref[pl.ds(first, rows + 2 * EDGE), :]
                exact = window.astype(F32)
                sums = [None, None]
                for tap in range(2 * half, 2 * half + 3):
                    if tap == 2:
                        shifted = window[EDGE : EDGE + rows]
                    else:
                        shifted = exact[EDGE + 2 - tap : EDGE + 2 - tap + rows].astype(BF16)
                    slots = [v for v in range(5) if TAPS[half][v][0] == tap]
                    term = lax.dot_general(
                        weights[slots[0] * unit : (slots[-1] + 1) * unit, :],
                        shifted,
                        (((1,), (1,)), ((), ())),
                        preferred_element_type=F32,
                    )
                    for k, v in enumerate(slots):
                        which = TAPS[half][v][1]
                        one = term[k * unit : (k + 1) * unit]
                        sums[which] = one if sums[which] is None else sums[which] + one
                for which in range(2):
                    out_ref[(n // 2) ^ half, which ^ half, n % 2] = sums[which].astype(out_ref.dtype)


def away_kernel(rows, unit, most_ref, dz_last, *refs):
    first, last, along_z, along_y, dz_ref, weights, out_ref = refs
    _, zl, y, _, _ = coords()
    place_dz(rows, dz_ref, 7)[...] = dz_last[...]
    units = (
        (0, first, 0),
        (4, last, 0),
        (2, along_z, 0),
        (1 + 2 * y, along_z, unit),
        (3 - 2 * y, along_y, rows),
    )
    for m, ref, start in units:
        slot = lax.rem(2 * zl + y + 5 - m, 5)
        weights[pl.ds(pl.multiple_of(slot * unit, EDGE), unit), :] = ref[start : start + unit]
    input_terms(rows, unit, dz_ref, weights, out_ref, 1)


def keep_kernel(rows, unit, dz_ref, weights, out_ref):
    input_terms(rows, unit, dz_ref, weights, out_ref, 0)


def cores_kernel(a, keep_ref, came_ref, keep_out, away_out):
    x = coords()[3]
    keep_out[...] = keep_ref[a, x] + came_ref[a, x].astype(F32)
    away_out[...] = (keep_ref[a, 1 - x] + came_ref[a, 1 - x].astype(F32)).astype(BF16)


def owners_kernel(keep_ref, came_ref, *out_refs):
    y = coords()[2]
    for b, ref in enumerate(out_refs):
        ref[...] = (keep_ref[y ^ b] + came_ref[y ^ b].astype(F32)).astype(BF16)


def last_kernel(unit, *refs):
    y, out_ref = coords()[2], refs[4]
    for b in range(2):
        first = pl.multiple_of((y ^ b) * unit, 16)
        out_ref[pl.ds(first, unit), :] = (refs[1 - b][...].astype(F32) + refs[3 - b][...].astype(F32)).astype(BF16)


def filter_kernel(scale, rows, own_ref, came_ref, dz_ref, first_ref, s1_ref, s2_ref, s3_ref, last_ref, lines, grads):
    h, zl, y, x, c = coords()
    unit, total = first_ref.shape[0], 8 * rows
    for cr, ref in enumerate((own_ref, came_ref)):
        for n in range(8):
            which = x ^ (n // 4) ^ h
            block = 4 * (h ^ (n // 2 % 2)) + 2 * (c ^ cr) + (y ^ (n % 2))
            lines[which, :, pl.ds(pl.multiple_of(block * rows, rows), rows)] = ref[n].astype(F32)
    lines[:, :, total:] = jnp.zeros((2, unit, lines.shape[2] - total), F32)
    for half in range(2):

        @pl.when(h == half)
        def _():
            for v, (tap, which) in enumerate(TAPS[half]):
                line = lines[which]
                if tap != 2:
                    line = pltpu.roll(line, (2 - tap) % lines.shape[2], 1)
                left = line[:, :total].astype(BF16)
                grads[v] = jnp.dot(left, dz_ref[EDGE:-EDGE, :], preferred_element_type=F32) * scale

    units = (0, 3 - 2 * y, 2, 1 + 2 * y, 4)
    for m, ref in zip(units, (first_ref, s1_ref, s2_ref, s3_ref, last_ref)):
        ref[...] = grads[lax.rem(2 * zl + y + 5 - m, 5)].astype(ref.dtype)


def home_kernel(unit, first_ref, zy_ref, z_ref, y_ref, last_ref, out_ref):
    y = coords()[2]
    for m, ref in ((0, first_ref), (1 + 2 * y, y_ref), (2, z_ref), (3 - 2 * y, zy_ref), (4, last_ref)):
        out_ref[pl.ds(pl.multiple_of(m * unit, 16), unit), :] = ref[...].astype(F32)


def call(kernel, name, shapes, args, scratch=(), flops=0, mib=16, anywhere=False, alias={}):
    many = isinstance(shapes, tuple)
    spec = pl.BlockSpec(memory_space=pltpu.VMEM)
    nbytes = sum(a.size * a.dtype.itemsize for a in args + (shapes if many else (shapes,)))
    return pl.pallas_call(
        kernel,
        out_shape=shapes,
        in_specs=[pl.BlockSpec(memory_space=pl.ANY) if anywhere else spec] * len(args),
        out_specs=(spec,) * len(shapes) if many else spec,
        scratch_shapes=list(scratch),
        input_output_aliases=alias,
        compiler_params=pltpu.CompilerParams(vmem_limit_bytes=mib << 20),
        cost_estimate=pl.CostEstimate(flops=0, bytes_accessed=1024, transcendentals=0),
        name=name,
    )(*args)


def shards_block(acts, pre_act, emb_grad, filters):
    rows, c_in = acts.shape
    wide = filters.shape[1]
    unit = c_in // 8
    total = 8 * rows
    flops = 2 * total * 5 * unit * wide
    shape = jax.ShapeDtypeStruct
    block, weight, pos = shape((rows, wide), BF16), shape((unit, wide), BF16), shape((unit, rows), BF16)

    tie = lax.optimization_barrier
    dz, along = call(
        dz_kernel,
        "dz",
        (block, shape((rows + 2 * unit, wide), BF16)),
        (pre_act, emb_grad, filters),
        scratch=[
            pltpu.VMEM(pre_act.shape, BF16),
            pltpu.VMEM(emb_grad.shape, BF16),
            pltpu.VMEM((2, unit, wide), BF16),
            pltpu.SemaphoreType.DMA((4,)),
        ],
        mib=60,
        anywhere=True,
    )
    own0, own1 = call(functools.partial(cut_kernel, unit), "cut", (pos, pos), (acts,), [pltpu.VMEM((rows, 512), BF16), pltpu.SemaphoreType.DMA], mib=60, anywhere=True)
    dz_h, dz_z, dz_y = send(dz, SWAP_H), send(dz, SWAP_Z), send(along, SWAP_Y)
    t01, t00 = send(own1, turn(0, 1)), send(own0, turn(0, 0))
    dz_zy = send(dz_z, SWAP_Y)
    near_got = call(join_kernel, "join_near", shape((2, unit, rows), BF16), (t00, t01), mib=4)
    far_got = send(near_got, SWAP_H)
    dz_h, dz_y, filters = tie((dz_h, dz_y, filters))
    dz_hz, dz_hy = send(dz_h, SWAP_Z), send(dz_h, SWAP_Y)

    w0, w4, along = call(
        functools.partial(units_kernel, unit),
        "units",
        (weight, weight, shape((2 * unit, wide), BF16)),
        (filters, dz_y),
        mib=4,
    )
    dz_hz, dz_zy, dz_hy, along, far_got = tie((dz_hz, dz_zy, dz_hy, along, far_got))
    got = call(join_kernel, "join", shape((2, 2, unit, rows), BF16), (near_got, far_got), mib=4)
    got = got.reshape(4, unit, rows)
    other = send(got, SWAP_X)
    dz_hzy = send(dz_hz, SWAP_Y)
    along = send(along, SWAP_Z)

    weights = (w0, w4, along, dz_y)
    dz_hzy, other, *weights = tie((dz_hzy, other, *weights))
    both = call(pair_kernel, "pair", shape((8, unit, rows), BF16), (got, other), mib=8)
    far_both = send(both, SWAP_C)
    padded = shape((total + 2 * EDGE, wide), BF16)
    most = call(
        functools.partial(gather_kernel, rows),
        "gather",
        padded,
        (dz, dz_y, dz_z, dz_zy, dz_h, dz_hy, dz_hz),
        mib=8,
    )
    dz_all, ordered, away = call(
        functools.partial(away_kernel, rows, unit),
        "away",
        (padded, shape((5 * unit, wide), BF16), shape((2, 2, 2, unit, rows), BF16)),
        (most, dz_hzy) + tuple(weights),
        flops=flops // 2,
        alias={0: 0},
    )
    keep = call(
        functools.partial(keep_kernel, rows, unit),
        "keep",
        shape((2, 2, 2, unit, rows), F32),
        (dz_all, ordered),
        flops=flops // 2,
    )

    came = send(away, SWAP_C)
    parts = (shape((2, unit, rows), F32), shape((2, unit, rows), BF16))
    keep_far, far = call(functools.partial(cores_kernel, 1), "cores_far", parts, (keep, came))
    keep, came, keep_far = tie((keep, came, keep_far))
    keep_near, near = call(functools.partial(cores_kernel, 0), "cores_near", parts, (keep, came))
    far, near = send(far, SWAP_X), send(near, SWAP_X)
    far_blocks = call(owners_kernel, "far", (pos,) * 2, (keep_far, far), mib=8)
    near_blocks = call(owners_kernel, "near", (pos,) * 2, (keep_near, near), mib=8)
    far_blocks = [send(block, turn(1, b)) for b, block in enumerate(far_blocks)]
    near_blocks = [send(block, turn(0, b)) for b, block in enumerate(near_blocks)]
    came = tuple(far_blocks[::-1] + near_blocks[::-1])
    input_grad = call(functools.partial(last_kernel, unit), "last", shape((2 * unit, rows), BF16), came, mib=4).T

    grads = call(
        functools.partial(filter_kernel, 1.0 / math.sqrt(total), rows),
        "filter",
        tuple(shape((unit, wide), F32 if m in (0, 4) else BF16) for m in range(5)),
        (both, far_both, dz_all),
        scratch=[pltpu.VMEM((2, unit, total + 128), F32), pltpu.VMEM((5, unit, wide), F32)],
        flops=flops,
    )
    first, along_y, along_z, across, last = grads
    grads = (first, send(across, SWAP_ZY), send(along_z, SWAP_Z), send(along_y, SWAP_Y), last)
    filter_grad = call(functools.partial(home_kernel, unit), "home", shape((5 * unit, wide), F32), grads, mib=8)
    return input_grad, filter_grad


def solution(mesh):
    in_specs = (P("seq", None), P("seq", "section"), P("seq", "section"), P("seq", "section"))
    out_specs = (P("seq", "section"), P("seq", "section"))
    block = mesh.shape["seq"] == 8 and mesh.shape["section"] == 4
    body = shards_block if block else shards_any
    return jax.shard_map(body, mesh=mesh, in_specs=in_specs, out_specs=out_specs, check_vma=False)
```
